128 devices in a mesh: grp: 4 (over y), lane: 32 (over x, z, core).
Axes of the slice: x: 4, y: 4, z: 4, core: 2. Of those that a mesh axis runs over, the one named last changes fastest.
Arguments:
- activations: bfloat16 [131072, 8192], P(('grp', 'lane')), may hold values from -60 to 60
- sketch: bfloat16 [8192, 256], replicated, may hold values from -0.0625 to 0.0625
Outputs:
- projection: float32 [8192, 256], P('lane')
The draws below stay inside these ranges and needn't reach their ends.
All inputs are finite; a program needn't handle non-finite values.
Results may differ from the reference program's by a relative error of at most 0.00068.
Values sent between devices are 32-bit elements; how exact they have to be, the bound alone decides.
A program may use at most 128 MiB of HBM per device.

```python
import math
import jax
import jax.numpy as jnp
from jax import lax

D = 8192
K = 256
ROWS = 131072


def draw_activations(key, part):
    key = jax.random.fold_in(key, 11)
    key_col, key_row, key_base = jax.random.split(key, 3)
    col_scale = jnp.exp(jax.random.uniform(key_col, (1, D), jnp.float32, math.log(0.3), math.log(3.0)))
    row_scale = jnp.exp(jax.random.uniform(key_row, (ROWS, 1), jnp.float32, math.log(0.5), math.log(2.0)))
    rising = 0.5 + jnp.arange(ROWS, dtype=jnp.float32)[:, None] / ROWS
    base = jnp.clip(jax.random.normal(key_base, (ROWS, D), jnp.float32), -6.0, 6.0)
    return (base * row_scale * rising * col_scale).astype(jnp.bfloat16)


def scatter_about(rng, extent, scale, limit, held_as=jnp.bfloat16):
    return jnp.clip(scale * jax.random.normal(rng, extent, jnp.float32), -limit, limit).astype(held_as)


def setup_inputs(seed: int = 0) -> dict:
    arg_keys = jax.random.split(jax.random.key(seed), 3)
    return {
        "activations": draw_activations(jax.random.fold_in(arg_keys[2], 71), 0),
        "sketch": scatter_about(arg_keys[1], (D, K), D ** -0.5, 0.0625),
    }


def reference(activations, sketch):
    sampled = jnp.dot(activations.astype(jnp.float32), sketch.astype(jnp.float32), preferred_element_type=jnp.float32)
    sampled_half = sampled.astype(jnp.bfloat16)
    gram = jnp.dot(sampled.T, sampled, precision=lax.Precision.HIGHEST)
    lower = jnp.linalg.cholesky(gram)
    cross = jnp.dot(activations.T.astype(jnp.float32), sampled_half.astype(jnp.float32), preferred_element_type=jnp.float32)
    return lax.linalg.triangular_solve(lower, cross, left_side=False, lower=True, transpose_a=True)
```

```python
import functools

import jax
import jax.numpy as jnp
from jax import lax
from jax.experimental import pallas as pl
from jax.experimental.pallas import tpu as pltpu
from jax.sharding import PartitionSpec as P

MESH = pl.DeviceIdType.MESH
F32, BF16 = jnp.float32, jnp.bfloat16
NK, KW = 8, 1024
RX, RZ, RY = 80, 80, 96
Y0, HXZ, HY, HY1 = RX + RZ, (RX + RZ) // 2, RY // 2, RY // 4


def mod4(v):
    return lax.rem(v, 4)


def wait(ref, sem):
    pltpu.make_async_copy(ref, ref, sem).wait()


def kernel(
    a_hbm, s_hbm, c_out, g_out,
    a, s, acc, ht, g, gh, gr, gy, gf, q, r, p, cb,
    rx, rz, ry, rx2, rz2, ry1, ry2, rq3, ry13, ry23,
    asem, ssem, gsem, qsem, rsem, ss1, rs1, ss2, rs2, ss3, rs3, ss4, rs4,
):
    y, lane = lax.axis_index("grp"), lax.axis_index("lane")
    x, z, c = lax.div(lane, 8), mod4(lax.div(lane, 2)), lax.rem(lane, 2)

    def dev(x_, y_, z_, c_):
        return {"grp": y_, "lane": (x_ * 4 + z_) * 2 + c_}

    def send(src, dst, ss, rs, to):
        pltpu.make_async_remote_copy(
            src_ref=src, dst_ref=dst, send_sem=ss, recv_sem=rs, device_id=to, device_id_type=MESH
        ).start()

    def load(i):
        cols = pl.ds(i * KW, KW)
        return (
            pltpu.make_async_copy(s_hbm.at[cols, :], s.at[cols, :], ssem.at[i]),
            pltpu.make_async_copy(a_hbm.at[:, cols], a.at[:, cols], asem.at[i]),
        )

    for i in range(NK):
        for copy in load(i):
            copy.start()

    barrier = pltpu.get_barrier_semaphore()
    pl.semaphore_signal(barrier, inc=1, device_id=dev(x, y, z, 1 - c), device_id_type=MESH)

    def greet(d, carry):
        to = dev(mod4(x + lax.div(d, 4)), y, mod4(z + lax.rem(d, 4)), c)
        pl.semaphore_signal(barrier, inc=1, device_id=to, device_id_type=MESH)
        return carry

    lax.fori_loop(1, 16, greet, 0)
    for d in range(1, 4):
        pl.semaphore_signal(barrier, inc=1, device_id=dev(x, mod4(y + d), z, c), device_id_type=MESH)

    acc[...] = jnp.zeros_like(acc)

    def sample(i, carry):
        cols = pl.ds(pl.multiple_of(i * KW, KW), KW)
        for copy in load_dyn(cols, i):
            copy.wait()
        acc[...] += jnp.dot(a[:, cols], s[cols, :], preferred_element_type=F32)
        return carry

    def load_dyn(cols, i):
        return (
            pltpu.make_async_copy(s_hbm.at[cols, :], s.at[cols, :], ssem.at[i]),
            pltpu.make_async_copy(a_hbm.at[:, cols], a.at[:, cols], asem.at[i]),
        )

    lax.fori_loop(0, NK, sample, 0)

    def mm(u, v):
        return jnp.dot(u, v, preferred_element_type=F32)

    def split(i, carry):
        g0, m = carry
        rows = pl.ds(pl.multiple_of(i * 256, 256), 256)
        v = acc[rows, :]
        hi = v.astype(BF16)
        rest = v - hi.astype(F32)
        mid = rest.astype(BF16)
        lo = (rest - mid.astype(F32)).astype(BF16)
        hit = hi.astype(F32).T.astype(BF16)
        ht[:, rows] = hit
        g0 = g0 + mm(hit, hi) + mm(mid.astype(F32).T.astype(BF16), mid)
        return g0, m + mm(hit, mid) + mm(hit, lo)

    zero = jnp.zeros((256, 256), F32)
    g0, m = lax.fori_loop(0, 4, split, (zero, zero))
    g[...] = g0 + m + m.T

    pl.semaphore_wait(barrier, 19)
    other = pl.ds(pl.multiple_of((1 - c) * 128, 128), 128)
    mine = pl.ds(pl.multiple_of(c * 128, 128), 128)
    core = dev(x, y, z, 1 - c)
    send(g.at[other, :], gh, gsem.at[0], gsem.at[1], core)

    def order(t):
        dx, dz = mod4(t + 1), mod4(lax.div(t, 4) + t + 1)
        return dx, dz, mod4(x + dx), mod4(z + dz)

    def block(x_, z_, c_):
        lb = (x_ * 4 + z_) * 2 + c_
        return mm(ht[...], a[:, pl.ds(pl.multiple_of(lb * 256, 256), 256)])

    def give(t, carry):
        _, _, x_, z_ = order(t)
        b = block(x_, z_, 1 - c)
        q[x_, z_, 0] = b[:, :128]
        q[x_, z_, 1] = b[:, 128:]
        send(q.at[x_, z_], r.at[x_, z_], qsem.at[x_ * 4 + z_], rsem.at[x_ * 4 + z_], core)
        return carry

    lax.fori_loop(0, 16, give, 0)

    wait(gh, gsem.at[1])
    g[mine, :] += gh[...]

    def piece(x_, z_):
        return pl.ds(pl.multiple_of(c * 128 + (x_ * 4 + z_) * 8, 8), 8)

    def scatter_gram(d, carry):
        x_, z_ = mod4(x + lax.div(d, 4)), mod4(z + lax.rem(d, 4))
        send(g.at[piece(x_, z_), :], gr.at[d - 1], gsem.at[2], gsem.at[3], dev(x_, y, z_, c))
        return carry

    lax.fori_loop(1, 16, scatter_gram, 0)

    def own(t, carry):
        dx, dz, x_, z_ = order(t)
        b = block(x_, z_, c)
        wait(r.at[x_, z_], rsem.at[x_ * 4 + z_])
        p[x_, z_, 0] = b[:, :128] + r[x_, z_, 0]
        p[x_, z_, 1] = b[:, 128:] + r[x_, z_, 1]

        @pl.when(dx != 0)
        def _():
            send(p.at[x_, z_, :, pl.ds(0, RX), :], rx.at[dx - 1, z_], ss1.at[dx - 1], rs1.at[dx - 1], dev(x_, y, z, c))

        @pl.when(dz != 0)
        def _():
            send(p.at[x_, z_, :, pl.ds(RX, RZ), :], rz.at[dz - 1, x_], ss1.at[dz + 2], rs1.at[dz + 2], dev(x, y, z_, c))

        for d in range(1, 4):
            y_ = mod4(y + d)
            rows = pl.ds(pl.multiple_of(Y0 + lax.div(y_, 2) * HY, 8), HY)
            send(p.at[x_, z_, lax.rem(y_, 2), rows, :], ry.at[d - 1, x_, z_], ss1.at[5 + d], rs1.at[5 + d], dev(x, y_, z, c))
        return carry

    lax.fori_loop(0, 16, own, 0)

    wait(gr, gsem.at[3])
    gy[y] = g[piece(x, z), :] + jnp.sum(gr[...], axis=0)
    for d in range(1, 4):
        send(gy.at[y], gy.at[y], gsem.at[4], gsem.at[5], dev(x, mod4(y + d), z, c))
    wait(gy.at[pl.ds(0, 3)], gsem.at[5])
    gf[piece(x, z), :] = (gy[0] + gy[1]) + (gy[2] + gy[3])

    def gather_gram(d, carry):
        x_, z_ = mod4(x + lax.div(d, 4)), mod4(z + lax.rem(d, 4))
        send(gf.at[piece(x, z), :], gf.at[piece(x, z), :], gsem.at[6], gsem.at[7], dev(x_, y, z_, c))
        return carry

    lax.fori_loop(1, 16, gather_gram, 0)

    ch = lax.rem(y, 2)
    y0 = Y0 + lax.div(y, 2) * HY
    rows_y = pl.ds(pl.multiple_of(y0, 8), HY)
    rows_1 = pl.ds(pl.multiple_of(y0, 8), HY1)
    rows_2 = pl.ds(pl.multiple_of(y0 + HY1, 8), HY - HY1)
    rows_x, rows_z = pl.ds(0, RX), pl.ds(RX, RZ)
    for d in range(3):
        wait(rx.at[d], rs1.at[d])
    for k in range(4):
        p[x, k, :, rows_x, :] += rx[0, k] + rx[1, k] + rx[2, k]
    for d in range(1, 4):
        z_ = mod4(z + d)
        send(p.at[x, z_, :, rows_x, :], rx2.at[d - 1], ss2.at[d - 1], rs2.at[d - 1], dev(x, y, z_, c))
    for d in range(3):
        wait(rz.at[d], rs1.at[3 + d])
    for k in range(4):
        p[k, z, :, rows_z, :] += rz[0, k] + rz[1, k] + rz[2, k]
    for d in range(1, 4):
        x_ = mod4(x + d)
        send(p.at[x_, z, :, rows_z, :], rz2.at[d - 1], ss2.at[2 + d], rs2.at[2 + d], dev(x_, y, z, c))
    for d in range(3):
        wait(ry.at[d], rs1.at[6 + d])
    for k in range(4):
        p[k, :, ch, rows_y, :] += ry[0, k] + ry[1, k] + ry[2, k]
    for d in range(1, 4):
        x_, z_ = mod4(x + d), mod4(z + d)
        send(p.at[x_, :, ch, rows_1, :], ry1.at[d - 1], ss2.at[5 + d], rs2.at[5 + d], dev(x_, y, z, c))
        send(p.at[:, z_, ch, rows_2, :], ry2.at[d - 1], ss2.at[8 + d], rs2.at[8 + d], dev(x, y, z_, c))

    wait(gf.at[pl.ds(0, 120), :], gsem.at[7])
    send(gf.at[mine, :], gf.at[mine, :], gsem.at[8], gsem.at[9], core)

    for d in range(3):
        wait(rx2.at[d], rs2.at[d])
    p[x, z, :, rows_x, :] += rx2[0] + rx2[1] + rx2[2]
    for d in range(3):
        wait(rz2.at[d], rs2.at[3 + d])
    p[x, z, :, rows_z, :] += rz2[0] + rz2[1] + rz2[2]
    for d in range(1, 4):
        y_ = mod4(y + d)
        rows = pl.ds(pl.multiple_of(lax.div(y_, 2) * HXZ, 8), HXZ)
        send(p.at[x, z, lax.rem(y_, 2), rows, :], rq3.at[d - 1], ss3.at[d - 1], rs3.at[d - 1], dev(x, y_, z, c))
    for d in range(3):
        wait(ry1.at[d], rs2.at[6 + d])
    p[x, :, ch, rows_1, :] += ry1[0] + ry1[1] + ry1[2]
    for d in range(1, 4):
        z_ = mod4(z + d)
        send(p.at[x, z_, ch, rows_1, :], ry13.at[d - 1], ss3.at[2 + d], rs3.at[2 + d], dev(x, y, z_, c))
    for d in range(3):
        wait(ry2.at[d], rs2.at[9 + d])
    p[:, z, ch, rows_2, :] += ry2[0] + ry2[1] + ry2[2]
    for d in range(1, 4):
        x_ = mod4(x + d)
        send(p.at[x_, z, ch, rows_2, :], ry23.at[d - 1], ss3.at[5 + d], rs3.at[5 + d], dev(x_, y, z, c))

    rows_q = pl.ds(pl.multiple_of(lax.div(y, 2) * HXZ, 8), HXZ)
    for d in range(3):
        wait(rq3.at[d], rs3.at[d])
    cb[ch, rows_q, :] = p[x, z, ch, rows_q, :] + (rq3[0] + rq3[1] + rq3[2])
    for d in range(1, 4):
        send(cb.at[ch, rows_q, :], cb.at[ch, rows_q, :], ss4.at[d - 1], rs4.at[d - 1], dev(x, mod4(y + d), z, c))
    for d in range(3):
        wait(ry13.at[d], rs3.at[3 + d])
        wait(ry23.at[d], rs3.at[6 + d])
    cb[ch, rows_1, :] = p[x, z, ch, rows_1, :] + (ry13[0] + ry13[1] + ry13[2])
    cb[ch, rows_2, :] = p[x, z, ch, rows_2, :] + (ry23[0] + ry23[1] + ry23[2])
    for d in range(1, 4):
        send(cb.at[ch, rows_y, :], cb.at[ch, rows_y, :], ss4.at[d + 2], rs4.at[d + 2], dev(x, mod4(y + d), z, c))

    def sent(t, carry):
        x_, z_ = lax.div(t, 4), lax.rem(t, 4)
        wait(q.at[x_, z_], qsem.at[t])
        return carry

    lax.fori_loop(0, 16, sent, 0)
    wait(gh, gsem.at[0])
    wait(gr, gsem.at[2])
    wait(gy.at[pl.ds(0, 3)], gsem.at[4])
    wait(gf.at[pl.ds(0, 120), :], gsem.at[6])
    wait(gf.at[mine, :], gsem.at[8])
    for d in range(3):
        wait(rx.at[d], ss1.at[d])
        wait(rz.at[d], ss1.at[3 + d])
        wait(ry.at[d], ss1.at[6 + d])
        wait(rx2.at[d], ss2.at[d])
        wait(rz2.at[d], ss2.at[3 + d])
        wait(ry1.at[d], ss2.at[6 + d])
        wait(ry2.at[d], ss2.at[9 + d])
        wait(rq3.at[d], ss3.at[d])
        wait(ry13.at[d], ss3.at[3 + d])
        wait(ry23.at[d], ss3.at[6 + d])
        wait(rq3.at[d], ss4.at[d])
        wait(cb.at[ch, rows_y, :], ss4.at[3 + d])
    wait(gf.at[other, :], gsem.at[9])
    g_out[...] = gf[...]
    for d in range(3):
        wait(rq3.at[d], rs4.at[d])
        wait(cb.at[ch, rows_y, :], rs4.at[3 + d])
    c_out[...] = cb[...]


def local(activations, sketch):
    dma = pltpu.SemaphoreType.DMA
    vmem = pltpu.VMEM
    crossed, gram = pl.pallas_call(
        kernel,
        out_shape=(jax.ShapeDtypeStruct((2, 256, 128), F32), jax.ShapeDtypeStruct((256, 256), F32)),
        in_specs=[pl.BlockSpec(memory_space=pl.ANY)] * 2,
        out_specs=[pl.BlockSpec(memory_space=pltpu.VMEM)] * 2,
        scratch_shapes=[
            vmem((1024, 8192), BF16), vmem((8192, 256), BF16), vmem((1024, 256), F32), vmem((256, 1024), BF16),
            vmem((256, 256), F32), vmem((128, 256), F32), vmem((15, 8, 256), F32), vmem((4, 8, 256), F32), vmem((256, 256), F32),
            vmem((4, 4, 2, 256, 128), F32), vmem((4, 4, 2, 256, 128), F32), vmem((4, 4, 2, 256, 128), F32), vmem((2, 256, 128), F32),
            vmem((3, 4, 2, RX, 128), F32), vmem((3, 4, 2, RZ, 128), F32), vmem((3, 4, 4, HY, 128), F32),
            vmem((3, 2, RX, 128), F32), vmem((3, 2, RZ, 128), F32), vmem((3, 4, HY1, 128), F32), vmem((3, 4, HY - HY1, 128), F32),
            vmem((3, HXZ, 128), F32), vmem((3, HY1, 128), F32), vmem((3, HY - HY1, 128), F32),
            dma((NK,)), dma((NK,)), dma((10,)), dma((16,)), dma((16,)),
            dma((9,)), dma((9,)), dma((12,)), dma((12,)), dma((9,)), dma((9,)), dma((6,)), dma((6,)),
        ],
        compiler_params=pltpu.CompilerParams(collective_id=0, has_side_effects=True, vmem_limit_bytes=56 << 20),
        cost_estimate=pl.CostEstimate(flops=9_000_000_000, bytes_accessed=22_000_000, transcendentals=0),
    )(activations, sketch)
    lower = jnp.linalg.cholesky(gram)
    cross = jnp.concatenate([crossed[0].T, crossed[1].T], axis=0)
    return lax.linalg.triangular_solve(lower, cross, left_side=False, lower=True, transpose_a=True)


def solution(mesh):
    return jax.shard_map(
        local,
        mesh=mesh,
        in_specs=(P(("grp", "lane"), None), P()),
        out_specs=P("lane", None),
        check_vma=False,
    )
```

```python
import functools

import jax
import jax.numpy as jnp
from jax import lax
from jax.experimental import pallas as pl
from jax.experimental.pallas import tpu as pltpu
from jax.sharding import PartitionSpec as P

MESH = pl.DeviceIdType.MESH
F32, BF16 = jnp.float32, jnp.bfloat16
NK, KW = 8, 1024
RX, RZ, RY = 80, 80, 96
NB = 64
Y0, HXZ, HY, HY1 = RX + RZ, (RX + RZ) // 2, RY // 2, RY // 4


def mod4(v):
    return lax.rem(v, 4)


def wait(ref, sem):
    pltpu.make_async_copy(ref, ref, sem).wait()


def panel(rows, q):
    n = len(rows)
    top = rows[q]
    wide = top.shape
    at = 8 * q

    def lanes(v, k):
        return jnp.broadcast_to(v[:, at + k:at + k + 1], wide)

    def subl(v, k):
        return jnp.broadcast_to(v[k:k + 1, :], wide)

    cols = [lanes(top, k) for k in range(8)]
    a = {(l, k): subl(cols[k], l) for k in range(8) for l in range(k, 8)}
    below = {i: [lanes(rows[i], k) for k in range(8)] for i in range(q + 1, n)}
    b = [subl(top, k) for k in range(8)]
    inv = []
    for k in range(8):
        rs = lax.rsqrt(a[k, k])
        inv.append(rs)
        for l in range(k + 1, 8):
            a[l, k] = a[l, k] * rs
        for m in range(k + 1, 8):
            for l in range(m, 8):
                a[l, m] = a[l, m] - a[l, k] * a[m, k]
        b[k] = b[k] * rs
        for l in range(k + 1, 8):
            b[l] = b[l] - a[l, k] * b[k]
    if q + 1 < n:
        d = [None] * 8
        for k in reversed(range(8)):
            v = b[k]
            for l in range(7, k, -1):
                v = v - a[l, k] * d[l]
            d[k] = v * inv[k]
        for i in range(q + 1, n):
            v = rows[i]
            for k in reversed(range(8)):
                v = v - below[i][k] * d[k]
            rows[i] = v
    sub = lax.broadcasted_iota(jnp.int32, wide, 0)
    out = b[0]
    for k in range(1, 8):
        out = jnp.where(sub == k, b[k], out)
    return out


def mm32(u, v):
    return jnp.dot(u, v, precision=lax.Precision.HIGHEST, preferred_element_type=F32)


def factor_step(gm, em, j):
    lo, hi = j * NB, (j + 1) * NB
    eye = (
        lax.broadcasted_iota(jnp.int32, (NB, NB), 0) == lax.broadcasted_iota(jnp.int32, (NB, NB), 1)
    ).astype(F32)
    m = jnp.concatenate([gm[lo:hi, lo:hi], eye], axis=1)
    rows = [m[8 * i : 8 * i + 8, :] for i in range(NB // 8)]
    w = jnp.concatenate([panel(rows, q) for q in range(NB // 8)], axis=0)[:, NB:]
    if j:
        em[lo:hi, 0:lo] = mm32(w, em[lo:hi, 0:lo])
    em[lo:hi, lo:hi] = w
    if hi < 256:
        t = mm32(w, gm[lo:hi, hi:256])
        tt = t.T
        gm[hi:256, hi:256] -= mm32(tt, t)
        em[hi:256, 0:hi] -= mm32(tt, em[lo:hi, 0:hi])


def kernel(
    a_hbm, s_hbm, out,
    a, s, acc, ht, g, gh, gr, gy, gf, q, r, p, cb,
    rx, rz, ry, rx2, rz2, ry1, ry2, rq3, ry13, ry23, em,
    asem, ssem, gsem, qsem, rsem, ss1, rs1, ss2, rs2, ss3, rs3, ss4, rs4,
):
    y, lane = lax.axis_index("grp"), lax.axis_index("lane")
    x, z, c = lax.div(lane, 8), mod4(lax.div(lane, 2)), lax.rem(lane, 2)

    def dev(x_, y_, z_, c_):
        return {"grp": y_, "lane": (x_ * 4 + z_) * 2 + c_}

    def send(src, dst, ss, rs, to):
        pltpu.make_async_remote_copy(
            src_ref=src, dst_ref=dst, send_sem=ss, recv_sem=rs, device_id=to, device_id_type=MESH
        ).start()

    def load(i):
        cols = pl.ds(i * KW, KW)
        return (
            pltpu.make_async_copy(s_hbm.at[cols, :], s.at[cols, :], ssem.at[i]),
            pltpu.make_async_copy(a_hbm.at[:, cols], a.at[:, cols], asem.at[i]),
        )

    for i in range(NK):
        for copy in load(i):
            copy.start()

    barrier = pltpu.get_barrier_semaphore()
    pl.semaphore_signal(barrier, inc=1, device_id=dev(x, y, z, 1 - c), device_id_type=MESH)

    def greet(d, carry):
        to = dev(mod4(x + lax.div(d, 4)), y, mod4(z + lax.rem(d, 4)), c)
        pl.semaphore_signal(barrier, inc=1, device_id=to, device_id_type=MESH)
        return carry

    lax.fori_loop(1, 16, greet, 0)
    for d in range(1, 4):
        pl.semaphore_signal(barrier, inc=1, device_id=dev(x, mod4(y + d), z, c), device_id_type=MESH)

    acc[...] = jnp.zeros_like(acc)

    def sample(i, carry):
        cols = pl.ds(pl.multiple_of(i * KW, KW), KW)
        for copy in load_dyn(cols, i):
            copy.wait()
        acc[...] += jnp.dot(a[:, cols], s[cols, :], preferred_element_type=F32)
        return carry

    def load_dyn(cols, i):
        return (
            pltpu.make_async_copy(s_hbm.at[cols, :], s.at[cols, :], ssem.at[i]),
            pltpu.make_async_copy(a_hbm.at[:, cols], a.at[:, cols], asem.at[i]),
        )

    lax.fori_loop(0, NK, sample, 0)

    def mm(u, v):
        return jnp.dot(u, v, preferred_element_type=F32)

    def split(i, carry):
        g0, m = carry
        rows = pl.ds(pl.multiple_of(i * 256, 256), 256)
        v = acc[rows, :]
        hi = v.astype(BF16)
        rest = v - hi.astype(F32)
        mid = rest.astype(BF16)
        lo = (rest - mid.astype(F32)).astype(BF16)
        hit = hi.astype(F32).T.astype(BF16)
        ht[:, rows] = hit
        g0 = g0 + mm(hit, hi) + mm(mid.astype(F32).T.astype(BF16), mid)
        return g0, m + mm(hit, mid) + mm(hit, lo)

    zero = jnp.zeros((256, 256), F32)
    g0, m = lax.fori_loop(0, 4, split, (zero, zero))
    g[...] = g0 + m + m.T

    pl.semaphore_wait(barrier, 19)
    other = pl.ds(pl.multiple_of((1 - c) * 128, 128), 128)
    mine = pl.ds(pl.multiple_of(c * 128, 128), 128)
    core = dev(x, y, z, 1 - c)
    send(g.at[other, :], gh, gsem.at[0], gsem.at[1], core)

    def order(t):
        dx, dz = mod4(t + 1), mod4(lax.div(t, 4) + t + 1)
        return dx, dz, mod4(x + dx), mod4(z + dz)

    def block(x_, z_, c_):
        lb = (x_ * 4 + z_) * 2 + c_
        return mm(ht[...], a[:, pl.ds(pl.multiple_of(lb * 256, 256), 256)])

    def give(t, carry):
        _, _, x_, z_ = order(t)
        b = block(x_, z_, 1 - c)
        q[x_, z_, 0] = b[:, :128]
        q[x_, z_, 1] = b[:, 128:]
        send(q.at[x_, z_], r.at[x_, z_], qsem.at[x_ * 4 + z_], rsem.at[x_ * 4 + z_], core)
        return carry

    lax.fori_loop(0, 16, give, 0)

    wait(gh, gsem.at[1])
    g[mine, :] += gh[...]

    def piece(x_, z_):
        return pl.ds(pl.multiple_of(c * 128 + (x_ * 4 + z_) * 8, 8), 8)

    def scatter_gram(d, carry):
        x_, z_ = mod4(x + lax.div(d, 4)), mod4(z + lax.rem(d, 4))
        send(g.at[piece(x_, z_), :], gr.at[d - 1], gsem.at[2], gsem.at[3], dev(x_, y, z_, c))
        return carry

    lax.fori_loop(1, 16, scatter_gram, 0)

    def own(t, carry):
        dx, dz, x_, z_ = order(t)
        b = block(x_, z_, c)
        wait(r.at[x_, z_], rsem.at[x_ * 4 + z_])
        p[x_, z_, 0] = b[:, :128] + r[x_, z_, 0]
        p[x_, z_, 1] = b[:, 128:] + r[x_, z_, 1]

        @pl.when(dx != 0)
        def _():
            send(p.at[x_, z_, :, pl.ds(0, RX), :], rx.at[dx - 1, z_], ss1.at[dx - 1], rs1.at[dx - 1], dev(x_, y, z, c))

        @pl.when(dz != 0)
        def _():
            send(p.at[x_, z_, :, pl.ds(RX, RZ), :], rz.at[dz - 1, x_], ss1.at[dz + 2], rs1.at[dz + 2], dev(x, y, z_, c))

        for d in range(1, 4):
            y_ = mod4(y + d)
            rows = pl.ds(pl.multiple_of(Y0 + lax.div(y_, 2) * HY, 8), HY)
            send(p.at[x_, z_, lax.rem(y_, 2), rows, :], ry.at[d - 1, x_, z_], ss1.at[5 + d], rs1.at[5 + d], dev(x, y_, z, c))
        return carry

    lax.fori_loop(0, 16, own, 0)

    wait(gr, gsem.at[3])
    gy[y] = g[piece(x, z), :] + jnp.sum(gr[...], axis=0)
    for d in range(1, 4):
        send(gy.at[y], gy.at[y], gsem.at[4], gsem.at[5], dev(x, mod4(y + d), z, c))
    wait(gy.at[pl.ds(0, 3)], gsem.at[5])
    gf[piece(x, z), :] = (gy[0] + gy[1]) + (gy[2] + gy[3])

    def gather_gram(d, carry):
        x_, z_ = mod4(x + lax.div(d, 4)), mod4(z + lax.rem(d, 4))
        send(gf.at[piece(x, z), :], gf.at[piece(x, z), :], gsem.at[6], gsem.at[7], dev(x_, y, z_, c))
        return carry

    lax.fori_loop(1, 16, gather_gram, 0)

    ch = lax.rem(y, 2)
    y0 = Y0 + lax.div(y, 2) * HY
    rows_y = pl.ds(pl.multiple_of(y0, 8), HY)
    rows_1 = pl.ds(pl.multiple_of(y0, 8), HY1)
    rows_2 = pl.ds(pl.multiple_of(y0 + HY1, 8), HY - HY1)
    rows_x, rows_z = pl.ds(0, RX), pl.ds(RX, RZ)
    for d in range(3):
        wait(rx.at[d], rs1.at[d])
    for k in range(4):
        p[x, k, :, rows_x, :] += rx[0, k] + rx[1, k] + rx[2, k]
    for d in range(1, 4):
        z_ = mod4(z + d)
        send(p.at[x, z_, :, rows_x, :], rx2.at[d - 1], ss2.at[d - 1], rs2.at[d - 1], dev(x, y, z_, c))
    for d in range(3):
        wait(rz.at[d], rs1.at[3 + d])
    for k in range(4):
        p[k, z, :, rows_z, :] += rz[0, k] + rz[1, k] + rz[2, k]
    for d in range(1, 4):
        x_ = mod4(x + d)
        send(p.at[x_, z, :, rows_z, :], rz2.at[d - 1], ss2.at[2 + d], rs2.at[2 + d], dev(x_, y, z, c))
    for d in range(3):
        wait(ry.at[d], rs1.at[6 + d])
    for k in range(4):
        p[k, :, ch, rows_y, :] += ry[0, k] + ry[1, k] + ry[2, k]
    for d in range(1, 4):
        x_, z_ = mod4(x + d), mod4(z + d)
        send(p.at[x_, :, ch, rows_1, :], ry1.at[d - 1], ss2.at[5 + d], rs2.at[5 + d], dev(x_, y, z, c))
        send(p.at[:, z_, ch, rows_2, :], ry2.at[d - 1], ss2.at[8 + d], rs2.at[8 + d], dev(x, y, z_, c))

    wait(gf.at[pl.ds(0, 120), :], gsem.at[7])
    send(gf.at[mine, :], gf.at[mine, :], gsem.at[8], gsem.at[9], core)
    em[...] = jnp.zeros_like(em)
    wait(gf.at[pl.ds(0, 120), :], gsem.at[6])
    wait(gf.at[mine, :], gsem.at[8])
    wait(gf.at[other, :], gsem.at[9])
    factor_step(gf, em, 0)
    factor_step(gf, em, 1)

    for d in range(3):
        wait(rx2.at[d], rs2.at[d])
    p[x, z, :, rows_x, :] += rx2[0] + rx2[1] + rx2[2]
    for d in range(3):
        wait(rz2.at[d], rs2.at[3 + d])
    p[x, z, :, rows_z, :] += rz2[0] + rz2[1] + rz2[2]
    for d in range(1, 4):
        y_ = mod4(y + d)
        rows = pl.ds(pl.multiple_of(lax.div(y_, 2) * HXZ, 8), HXZ)
        send(p.at[x, z, lax.rem(y_, 2), rows, :], rq3.at[d - 1], ss3.at[d - 1], rs3.at[d - 1], dev(x, y_, z, c))
    for d in range(3):
        wait(ry1.at[d], rs2.at[6 + d])
    p[x, :, ch, rows_1, :] += ry1[0] + ry1[1] + ry1[2]
    for d in range(1, 4):
        z_ = mod4(z + d)
        send(p.at[x, z_, ch, rows_1, :], ry13.at[d - 1], ss3.at[2 + d], rs3.at[2 + d], dev(x, y, z_, c))
    for d in range(3):
        wait(ry2.at[d], rs2.at[9 + d])
    p[:, z, ch, rows_2, :] += ry2[0] + ry2[1] + ry2[2]
    for d in range(1, 4):
        x_ = mod4(x + d)
        send(p.at[x_, z, ch, rows_2, :], ry23.at[d - 1], ss3.at[5 + d], rs3.at[5 + d], dev(x_, y, z, c))

    factor_step(gf, em, 2)

    rows_q = pl.ds(pl.multiple_of(lax.div(y, 2) * HXZ, 8), HXZ)
    for d in range(3):
        wait(rq3.at[d], rs3.at[d])
    cb[ch, rows_q, :] = p[x, z, ch, rows_q, :] + (rq3[0] + rq3[1] + rq3[2])
    for d in range(1, 4):
        send(cb.at[ch, rows_q, :], cb.at[ch, rows_q, :], ss4.at[d - 1], rs4.at[d - 1], dev(x, mod4(y + d), z, c))
    for d in range(3):
        wait(ry13.at[d], rs3.at[3 + d])
        wait(ry23.at[d], rs3.at[6 + d])
    cb[ch, rows_1, :] = p[x, z, ch, rows_1, :] + (ry13[0] + ry13[1] + ry13[2])
    cb[ch, rows_2, :] = p[x, z, ch, rows_2, :] + (ry23[0] + ry23[1] + ry23[2])
    for d in range(1, 4):
        send(cb.at[ch, rows_y, :], cb.at[ch, rows_y, :], ss4.at[d + 2], rs4.at[d + 2], dev(x, mod4(y + d), z, c))

    factor_step(gf, em, 3)

    def sent(t, carry):
        x_, z_ = lax.div(t, 4), lax.rem(t, 4)
        wait(q.at[x_, z_], qsem.at[t])
        return carry

    lax.fori_loop(0, 16, sent, 0)
    wait(gh, gsem.at[0])
    wait(gr, gsem.at[2])
    wait(gy.at[pl.ds(0, 3)], gsem.at[4])
    for d in range(3):
        wait(rx.at[d], ss1.at[d])
        wait(rz.at[d], ss1.at[3 + d])
        wait(ry.at[d], ss1.at[6 + d])
        wait(rx2.at[d], ss2.at[d])
        wait(rz2.at[d], ss2.at[3 + d])
        wait(ry1.at[d], ss2.at[6 + d])
        wait(ry2.at[d], ss2.at[9 + d])
        wait(rq3.at[d], ss3.at[d])
        wait(ry13.at[d], ss3.at[3 + d])
        wait(ry23.at[d], ss3.at[6 + d])
        wait(rq3.at[d], ss4.at[d])
        wait(cb.at[ch, rows_y, :], ss4.at[3 + d])
    for d in range(3):
        wait(rq3.at[d], rs4.at[d])
        wait(cb.at[ch, rows_y, :], rs4.at[3 + d])
    for h in range(2):
        out[128 * h : 128 * h + 128, :] = mm32(em[...], cb[h]).T


def local(activations, sketch):
    dma = pltpu.SemaphoreType.DMA
    vmem = pltpu.VMEM
    return pl.pallas_call(
        kernel,
        out_shape=jax.ShapeDtypeStruct((256, 256), F32),
        in_specs=[pl.BlockSpec(memory_space=pl.ANY)] * 2,
        out_specs=pl.BlockSpec(memory_space=pltpu.VMEM),
        scratch_shapes=[
            vmem((1024, 8192), BF16), vmem((8192, 256), BF16), vmem((1024, 256), F32), vmem((256, 1024), BF16),
            vmem((256, 256), F32), vmem((128, 256), F32), vmem((15, 8, 256), F32), vmem((4, 8, 256), F32), vmem((256, 256), F32),
            vmem((4, 4, 2, 256, 128), F32), vmem((4, 4, 2, 256, 128), F32), vmem((4, 4, 2, 256, 128), F32), vmem((2, 256, 128), F32),
            vmem((3, 4, 2, RX, 128), F32), vmem((3, 4, 2, RZ, 128), F32), vmem((3, 4, 4, HY, 128), F32),
            vmem((3, 2, RX, 128), F32), vmem((3, 2, RZ, 128), F32), vmem((3, 4, HY1, 128), F32), vmem((3, 4, HY - HY1, 128), F32),
            vmem((3, HXZ, 128), F32), vmem((3, HY1, 128), F32), vmem((3, HY - HY1, 128), F32), vmem((256, 256), F32),
            dma((NK,)), dma((NK,)), dma((10,)), dma((16,)), dma((16,)),
            dma((9,)), dma((9,)), dma((12,)), dma((12,)), dma((9,)), dma((9,)), dma((6,)), dma((6,)),
        ],
        compiler_params=pltpu.CompilerParams(collective_id=0, has_side_effects=True, vmem_limit_bytes=56 << 20),
        cost_estimate=pl.CostEstimate(flops=9_000_000_000, bytes_accessed=22_000_000, transcendentals=0),
    )(activations, sketch)


def solution(mesh):
    return jax.shard_map(
        local,
        mesh=mesh,
        in_specs=(P(("grp", "lane"), None), P()),
        out_specs=P("lane", None),
        check_vma=False,
    )
```

```python
import functools

import jax
import jax.numpy as jnp
from jax import lax
from jax.experimental import pallas as pl
from jax.experimental.pallas import tpu as pltpu
from jax.sharding import PartitionSpec as P

MESH = pl.DeviceIdType.MESH
F32, BF16 = jnp.float32, jnp.bfloat16
NK, KW = 8, 1024
RX, RZ, RY = 80, 80, 96
NB = 64
Y0, HXZ, HY, HY1 = RX + RZ, (RX + RZ) // 2, RY // 2, 24


def mod4(v):
    return lax.rem(v, 4)


def wait(ref, sem):
    pltpu.make_async_copy(ref, ref, sem).wait()


def panel(rows, q):
    n = len(rows)
    top = rows[q]
    wide = top.shape
    at = 8 * q

    def lanes(v, k):
        return jnp.broadcast_to(v[:, at + k:at + k + 1], wide)

    def subl(v, k):
        return jnp.broadcast_to(v[k:k + 1, :], wide)

    cols = [lanes(top, k) for k in range(8)]
    a = {(l, k): subl(cols[k], l) for k in range(8) for l in range(k, 8)}
    below = {i: [lanes(rows[i], k) for k in range(8)] for i in range(q + 1, n)}
    b = [subl(top, k) for k in range(8)]
    inv = []
    for k in range(8):
        rs = lax.rsqrt(a[k, k])
        inv.append(rs)
        for l in range(k + 1, 8):
            a[l, k] = a[l, k] * rs
        for m in range(k + 1, 8):
            for l in range(m, 8):
                a[l, m] = a[l, m] - a[l, k] * a[m, k]
        b[k] = b[k] * rs
        for l in range(k + 1, 8):
            b[l] = b[l] - a[l, k] * b[k]
    if q + 1 < n:
        d = [None] * 8
        for k in reversed(range(8)):
            v = b[k]
            for l in range(7, k, -1):
                v = v - a[l, k] * d[l]
            d[k] = v * inv[k]
        for i in range(q + 1, n):
            v = rows[i]
            for k in reversed(range(8)):
                v = v - below[i][k] * d[k]
            rows[i] = v
    sub = lax.broadcasted_iota(jnp.int32, wide, 0)
    out = b[0]
    for k in range(1, 8):
        out = jnp.where(sub == k, b[k], out)
    return out


def mm32(u, v):
    return jnp.dot(u, v, precision=lax.Precision.HIGHEST, preferred_element_type=F32)


def factor_step(gm, em, j):
    lo, hi = j * NB, (j + 1) * NB
    eye = (
        lax.broadcasted_iota(jnp.int32, (NB, NB), 0) == lax.broadcasted_iota(jnp.int32, (NB, NB), 1)
    ).astype(F32)
    m = jnp.concatenate([gm[lo:hi, lo:hi], eye], axis=1)
    rows = [m[8 * i : 8 * i + 8, :] for i in range(NB // 8)]
    w = jnp.concatenate([panel(rows, q) for q in range(NB // 8)], axis=0)[:, NB:]
    if j:
        em[lo:hi, 0:lo] = mm32(w, em[lo:hi, 0:lo])
    em[lo:hi, lo:hi] = w
    if hi < 256:
        t = mm32(w, gm[lo:hi, hi:256])
        tt = t.T
        gm[hi:256, hi:256] -= mm32(tt, t)
        em[hi:256, 0:hi] -= mm32(tt, em[lo:hi, 0:hi])


def kernel(
    a_hbm, s_hbm, out,
    a, s, acc, ht, g, gh, gr, gy, gf, q, r, p, cb,
    rx, rz, ry, rx2, rz2, ry1, ry2, rq3, ry13, ry23, em,
    asem, ssem, gsem, qsem, rsem, ss1, rs1, ss2, rs2, ss3, rs3, ss4, rs4,
):
    y, lane = lax.axis_index("grp"), lax.axis_index("lane")
    x, z, c = lax.div(lane, 8), mod4(lax.div(lane, 2)), lax.rem(lane, 2)

    def dev(x_, y_, z_, c_):
        return {"grp": y_, "lane": (x_ * 4 + z_) * 2 + c_}

    def send(src, dst, ss, rs, to):
        pltpu.make_async_remote_copy(
            src_ref=src, dst_ref=dst, send_sem=ss, recv_sem=rs, device_id=to, device_id_type=MESH
        ).start()

    def load(i):
        cols = pl.ds(pl.multiple_of(i * KW, KW), KW)
        return (
            pltpu.make_async_copy(s_hbm.at[cols, :], s.at[cols, :], ssem.at[i]),
            pltpu.make_async_copy(a_hbm.at[:, cols], a.at[:, cols], asem.at[i]),
        )

    for i in range(NK):
        for copy in load(i):
            copy.start()

    barrier = pltpu.get_barrier_semaphore()
    pl.semaphore_signal(barrier, inc=1, device_id=dev(x, y, z, 1 - c), device_id_type=MESH)

    def greet(d, carry):
        to = dev(mod4(x + lax.div(d, 4)), y, mod4(z + lax.rem(d, 4)), c)
        pl.semaphore_signal(barrier, inc=1, device_id=to, device_id_type=MESH)
        return carry

    lax.fori_loop(1, 16, greet, 0)
    for d in range(1, 4):
        pl.semaphore_signal(barrier, inc=1, device_id=dev(x, mod4(y + d), z, c), device_id_type=MESH)

    acc[...] = jnp.zeros_like(acc)

    def sample(i, carry):
        cols = pl.ds(pl.multiple_of(i * KW, KW), KW)
        for copy in load(i):
            copy.wait()
        acc[...] += jnp.dot(a[:, cols], s[cols, :], preferred_element_type=F32)
        return carry

    lax.fori_loop(0, NK, sample, 0)

    def mm(u, v):
        return jnp.dot(u, v, preferred_element_type=F32)

    def split(i, carry):
        g0, m = carry
        rows = pl.ds(pl.multiple_of(i * 256, 256), 256)
        v = acc[rows, :]
        hi = v.astype(BF16)
        rest = v - hi.astype(F32)
        mid = rest.astype(BF16)
        lo = (rest - mid.astype(F32)).astype(BF16)
        hit = hi.astype(F32).T.astype(BF16)
        ht[:, rows] = hit
        g0 = g0 + mm(hit, hi) + mm(mid.astype(F32).T.astype(BF16), mid)
        return g0, m + mm(hit, mid) + mm(hit, lo)

    zero = jnp.zeros((256, 256), F32)
    g0, m = lax.fori_loop(0, 4, split, (zero, zero))
    g[...] = g0 + m + m.T

    pl.semaphore_wait(barrier, 19)
    other = pl.ds(pl.multiple_of((1 - c) * 128, 128), 128)
    mine = pl.ds(pl.multiple_of(c * 128, 128), 128)
    core = dev(x, y, z, 1 - c)
    send(g.at[other, :], gh, gsem.at[0], gsem.at[1], core)

    def piece(x_, z_):
        return pl.ds(pl.multiple_of(c * 128 + (x_ * 4 + z_) * 8, 8), 8)

    def plane(d):
        return mod4(x + lax.div(d, 4)), mod4(z + lax.rem(d, 4))

    def scatter_gram(d, carry):
        x_, z_ = plane(d)
        send(g.at[piece(x_, z_), :], gr.at[d - 1], gsem.at[2], gsem.at[3], dev(x_, y, z_, c))
        return carry

    def order(i, k):
        dx, dz = (k + 1) % 4, mod4(i + k + 1)
        return dx, dz, mod4(x + dx), mod4(z + dz)

    def block(x_, z_, c_):
        lb = (x_ * 4 + z_) * 2 + c_
        return mm(ht[...], a[:, pl.ds(pl.multiple_of(lb * 256, 256), 256)])

    def give(i):
        for k in range(4):
            _, _, x_, z_ = order(i, k)
            b = block(x_, z_, 1 - c)
            q[x_, z_, 0] = b[:, :128]
            q[x_, z_, 1] = b[:, 128:]
        for k in range(4):
            _, _, x_, z_ = order(i, k)
            send(q.at[x_, z_], r.at[x_, z_], qsem.at[x_ * 4 + z_], rsem.at[x_ * 4 + z_], core)

    def own(i):
        for k in range(4):
            _, _, x_, z_ = order(i, k)
            b = block(x_, z_, c)
            p[x_, z_, 0] = b[:, :128]
            p[x_, z_, 1] = b[:, 128:]
        for k in range(4):
            _, _, x_, z_ = order(i, k)
            wait(r.at[x_, z_], rsem.at[x_ * 4 + z_])
            p[x_, z_] += r[x_, z_]

    def scatter(i):
        for k in range(4):
            dx, dz, x_, z_ = order(i, k)
            if dx:
                send(p.at[x_, z_, :, pl.ds(0, RX), :], rx.at[dx - 1, z_], ss1.at[dx - 1], rs1.at[dx - 1], dev(x_, y, z, c))

            @pl.when(dz != 0)
            def _():
                send(p.at[x_, z_, :, pl.ds(RX, RZ), :], rz.at[dz - 1, x_], ss1.at[dz + 2], rs1.at[dz + 2], dev(x, y, z_, c))

            for d in range(1, 4):
                y_ = mod4(y + d)
                rows = pl.ds(pl.multiple_of(Y0 + lax.div(y_, 2) * HY, 8), HY)
                send(p.at[x_, z_, lax.rem(y_, 2), rows, :], ry.at[d - 1, x_, z_], ss1.at[5 + d], rs1.at[5 + d], dev(x, y_, z, c))

    def turn(i, carry):
        @pl.when(i < 4)
        def _():
            give(i)

        @pl.when(i == 1)
        def _():
            wait(gh, gsem.at[1])
            g[mine, :] += gh[...]
            lax.fori_loop(1, 16, scatter_gram, 0)

        @pl.when(i == 4)
        def _():
            wait(gr, gsem.at[3])
            gy[y] = g[piece(x, z), :] + jnp.sum(gr[...], axis=0)
            for d in range(1, 4):
                send(gy.at[y], gy.at[y], gsem.at[4], gsem.at[5], dev(x, mod4(y + d), z, c))
            scatter(1)

        @pl.when(i >= 1)
        def _():
            own(i - 1)

        @pl.when(i == 1)
        def _():
            scatter(0)

        return carry

    lax.fori_loop(0, 5, turn, 0)

    def gather_gram(d, carry):
        x_, z_ = plane(d)
        send(gf.at[piece(x, z), :], gf.at[piece(x, z), :], gsem.at[6], gsem.at[7], dev(x_, y, z_, c))
        return carry

    def rest(i, carry):
        scatter(i)
        return carry

    def sum_groups():
        wait(gy.at[pl.ds(0, 3)], gsem.at[5])
        gf[piece(x, z), :] = (gy[0] + gy[1]) + (gy[2] + gy[3])
        lax.fori_loop(1, 16, gather_gram, 0)
        lax.fori_loop(2, 4, rest, 0)

    def swap_halves():
        wait(gf.at[pl.ds(0, 120), :], gsem.at[7])
        send(gf.at[mine, :], gf.at[mine, :], gsem.at[8], gsem.at[9], core)
        em[...] = jnp.zeros_like(em)

    def halves():
        wait(gf.at[pl.ds(0, 120), :], gsem.at[6])
        wait(gf.at[mine, :], gsem.at[8])
        wait(gf.at[other, :], gsem.at[9])

    def f(j):
        return lambda: factor_step(gf, em, j)

    plan = {0: (sum_groups, swap_halves, halves, f(0)), 1: (f(1),), 2: (f(2),), 3: (f(3),), 4: ()}

    def slot(i):
        for step in plan[i]:
            step()

    slot(0)

    ch = lax.rem(y, 2)
    y0 = Y0 + lax.div(y, 2) * HY
    rows_y = pl.ds(pl.multiple_of(y0, 8), HY)
    rows_1 = pl.ds(pl.multiple_of(y0, 8), HY1)
    rows_2 = pl.ds(pl.multiple_of(y0 + HY1, 8), HY - HY1)
    rows_x, rows_z = pl.ds(0, RX), pl.ds(RX, RZ)
    for d in range(3):
        wait(rx.at[d], rs1.at[d])
    for k in range(4):
        p[x, k, :, rows_x, :] += rx[0, k] + rx[1, k] + rx[2, k]
    for d in range(1, 4):
        z_ = mod4(z + d)
        send(p.at[x, z_, :, rows_x, :], rx2.at[d - 1], ss2.at[d - 1], rs2.at[d - 1], dev(x, y, z_, c))
    for d in range(3):
        wait(rz.at[d], rs1.at[3 + d])
    for k in range(4):
        p[k, z, :, rows_z, :] += rz[0, k] + rz[1, k] + rz[2, k]
    for d in range(1, 4):
        x_ = mod4(x + d)
        send(p.at[x_, z, :, rows_z, :], rz2.at[d - 1], ss2.at[2 + d], rs2.at[2 + d], dev(x_, y, z, c))
    slot(1)
    for d in range(3):
        wait(ry.at[d], rs1.at[6 + d])
    for k in range(4):
        p[k, :, ch, rows_y, :] += ry[0, k] + ry[1, k] + ry[2, k]
    for d in range(1, 4):
        x_, z_ = mod4(x + d), mod4(z + d)
        send(p.at[x_, :, ch, rows_1, :], ry1.at[d - 1], ss2.at[5 + d], rs2.at[5 + d], dev(x_, y, z, c))
        send(p.at[:, z_, ch, rows_2, :], ry2.at[d - 1], ss2.at[8 + d], rs2.at[8 + d], dev(x, y, z_, c))

    slot(2)

    for d in range(3):
        wait(rx2.at[d], rs2.at[d])
    p[x, z, :, rows_x, :] += rx2[0] + rx2[1] + rx2[2]
    for d in range(3):
        wait(rz2.at[d], rs2.at[3 + d])
    p[x, z, :, rows_z, :] += rz2[0] + rz2[1] + rz2[2]
    for d in range(1, 4):
        y_ = mod4(y + d)
        rows = pl.ds(pl.multiple_of(lax.div(y_, 2) * HXZ, 8), HXZ)
        send(p.at[x, z, lax.rem(y_, 2), rows, :], rq3.at[d - 1], ss3.at[d - 1], rs3.at[d - 1], dev(x, y_, z, c))
    for d in range(3):
        wait(ry1.at[d], rs2.at[6 + d])
    p[x, :, ch, rows_1, :] += ry1[0] + ry1[1] + ry1[2]
    for d in range(1, 4):
        z_ = mod4(z + d)
        send(p.at[x, z_, ch, rows_1, :], ry13.at[d - 1], ss3.at[2 + d], rs3.at[2 + d], dev(x, y, z_, c))
    for d in range(3):
        wait(ry2.at[d], rs2.at[9 + d])
    p[:, z, ch, rows_2, :] += ry2[0] + ry2[1] + ry2[2]
    for d in range(1, 4):
        x_ = mod4(x + d)
        send(p.at[x_, z, ch, rows_2, :], ry23.at[d - 1], ss3.at[5 + d], rs3.at[5 + d], dev(x_, y, z, c))

    slot(3)

    rows_q = pl.ds(pl.multiple_of(lax.div(y, 2) * HXZ, 8), HXZ)
    for d in range(3):
        wait(rq3.at[d], rs3.at[d])
    cb[ch, rows_q, :] = p[x, z, ch, rows_q, :] + (rq3[0] + rq3[1] + rq3[2])
    for d in range(1, 4):
        send(cb.at[ch, rows_q, :], cb.at[ch, rows_q, :], ss4.at[d - 1], rs4.at[d - 1], dev(x, mod4(y + d), z, c))
    for d in range(3):
        wait(ry13.at[d], rs3.at[3 + d])
        wait(ry23.at[d], rs3.at[6 + d])
    cb[ch, rows_1, :] = p[x, z, ch, rows_1, :] + (ry13[0] + ry13[1] + ry13[2])
    cb[ch, rows_2, :] = p[x, z, ch, rows_2, :] + (ry23[0] + ry23[1] + ry23[2])
    for d in range(1, 4):
        send(cb.at[ch, rows_y, :], cb.at[ch, rows_y, :], ss4.at[d + 2], rs4.at[d + 2], dev(x, mod4(y + d), z, c))

    slot(4)

    def sent(t, carry):
        x_, z_ = lax.div(t, 4), lax.rem(t, 4)
        wait(q.at[x_, z_], qsem.at[t])
        return carry

    lax.fori_loop(0, 16, sent, 0)
    wait(gh, gsem.at[0])
    wait(gr, gsem.at[2])
    wait(gy.at[pl.ds(0, 3)], gsem.at[4])
    for d in range(3):
        wait(rx.at[d], ss1.at[d])
        wait(rz.at[d], ss1.at[3 + d])
        wait(ry.at[d], ss1.at[6 + d])
        wait(rx2.at[d], ss2.at[d])
        wait(rz2.at[d], ss2.at[3 + d])
        wait(ry1.at[d], ss2.at[6 + d])
        wait(ry2.at[d], ss2.at[9 + d])
        wait(rq3.at[d], ss3.at[d])
        wait(ry13.at[d], ss3.at[3 + d])
        wait(ry23.at[d], ss3.at[6 + d])
        wait(rq3.at[d], ss4.at[d])
        wait(cb.at[ch, rows_y, :], ss4.at[3 + d])
    for d in range(3):
        wait(rq3.at[d], rs4.at[d])
        wait(cb.at[ch, rows_y, :], rs4.at[3 + d])
    for h in range(2):
        out[:, 128 * h : 128 * h + 128] = mm32(em[...], cb[h])


def local(activations, sketch):
    dma = pltpu.SemaphoreType.DMA
    vmem = pltpu.VMEM
    return pl.pallas_call(
        kernel,
        out_shape=jax.ShapeDtypeStruct((256, 256), F32),
        in_specs=[pl.BlockSpec(memory_space=pl.ANY)] * 2,
        out_specs=pl.BlockSpec(memory_space=pltpu.VMEM),
        scratch_shapes=[
            vmem((1024, 8192), BF16), vmem((8192, 256), BF16), vmem((1024, 256), F32), vmem((256, 1024), BF16),
            vmem((256, 256), F32), vmem((128, 256), F32), vmem((15, 8, 256), F32), vmem((4, 8, 256), F32), vmem((256, 256), F32),
            vmem((4, 4, 2, 256, 128), F32), vmem((4, 4, 2, 256, 128), F32), vmem((4, 4, 2, 256, 128), F32), vmem((2, 256, 128), F32),
            vmem((3, 4, 2, RX, 128), F32), vmem((3, 4, 2, RZ, 128), F32), vmem((3, 4, 4, HY, 128), F32),
            vmem((3, 2, RX, 128), F32), vmem((3, 2, RZ, 128), F32), vmem((3, 4, HY1, 128), F32), vmem((3, 4, HY - HY1, 128), F32),
            vmem((3, HXZ, 128), F32), vmem((3, HY1, 128), F32), vmem((3, HY - HY1, 128), F32), vmem((256, 256), F32),
            dma((NK,)), dma((NK,)), dma((10,)), dma((16,)), dma((16,)),
            dma((9,)), dma((9,)), dma((12,)), dma((12,)), dma((9,)), dma((9,)), dma((6,)), dma((6,)),
        ],
        compiler_params=pltpu.CompilerParams(collective_id=0, has_side_effects=True, vmem_limit_bytes=56 << 20),
        cost_estimate=pl.CostEstimate(flops=9_000_000_000, bytes_accessed=22_000_000, transcendentals=0),
    )(activations, sketch).T


def solution(mesh):
    return jax.shard_map(
        local,
        mesh=mesh,
        in_specs=(P(("grp", "lane"), None), P()),
        out_specs=P("lane", None),
        check_vma=False,
    )
```

```python
import functools

import jax
import jax.numpy as jnp
from jax import lax
from jax.experimental import pallas as pl
from jax.experimental.pallas import tpu as pltpu
from jax.sharding import PartitionSpec as P

MESH = pl.DeviceIdType.MESH
F32, BF16 = jnp.float32, jnp.bfloat16
NK, KW = 8, 1024
RX, RZ, RY = 80, 80, 96
NB = 64
Y0, HXZ, HY, HY1 = RX + RZ, (RX + RZ) // 2, RY // 2, 24


def mod4(v):
    return lax.rem(v, 4)


def wait(ref, sem):
    pltpu.make_async_copy(ref, ref, sem).wait()


def panel(rows, q):
    n = len(rows)
    top = rows[q]
    wide = top.shape
    at = 8 * q

    def lanes(v, k):
        return jnp.broadcast_to(v[:, at + k:at + k + 1], wide)

    def subl(v, k):
        return jnp.broadcast_to(v[k:k + 1, :], wide)

    cols = [lanes(top, k) for k in range(8)]
    a = {(l, k): subl(cols[k], l) for k in range(8) for l in range(k, 8)}
    below = {i: [lanes(rows[i], k) for k in range(8)] for i in range(q + 1, n)}
    b = [subl(top, k) for k in range(8)]
    inv = []
    for k in range(8):
        rs = lax.rsqrt(a[k, k])
        inv.append(rs)
        for l in range(k + 1, 8):
            a[l, k] = a[l, k] * rs
        for m in range(k + 1, 8):
            for l in range(m, 8):
                a[l, m] = a[l, m] - a[l, k] * a[m, k]
        b[k] = b[k] * rs
        for l in range(k + 1, 8):
            b[l] = b[l] - a[l, k] * b[k]
    if q + 1 < n:
        d = [None] * 8
        for k in reversed(range(8)):
            v = b[k]
            for l in range(7, k, -1):
                v = v - a[l, k] * d[l]
            d[k] = v * inv[k]
        for i in range(q + 1, n):
            v = rows[i]
            for k in reversed(range(8)):
                v = v - below[i][k] * d[k]
            rows[i] = v
    sub = lax.broadcasted_iota(jnp.int32, wide, 0)
    out = b[0]
    for k in range(1, 8):
        out = jnp.where(sub == k, b[k], out)
    return out


def mm32(u, v):
    return jnp.dot(u, v, precision=lax.Precision.HIGHEST, preferred_element_type=F32)


def factor_step(gm, em, j):
    lo, hi = j * NB, (j + 1) * NB
    eye = (
        lax.broadcasted_iota(jnp.int32, (NB, NB), 0) == lax.broadcasted_iota(jnp.int32, (NB, NB), 1)
    ).astype(F32)
    m = jnp.concatenate([gm[lo:hi, lo:hi], eye], axis=1)
    rows = [m[8 * i : 8 * i + 8, :] for i in range(NB // 8)]
    w = jnp.concatenate([panel(rows, q) for q in range(NB // 8)], axis=0)[:, NB:]
    if j:
        em[lo:hi, 0:lo] = mm32(w, em[lo:hi, 0:lo])
    em[lo:hi, lo:hi] = w
    if hi < 256:
        t = mm32(w, gm[lo:hi, hi:256])
        tt = t.T
        gm[hi:256, hi:256] -= mm32(tt, t)
        em[hi:256, 0:hi] -= mm32(tt, em[lo:hi, 0:hi])


def kernel(
    a_hbm, s_hbm, out,
    a, s, acc, ht, g, gh, gr, gy, gf, q, r, p, cb,
    qx, qz, qy, rx, rz, ry, rx2, rz2, ry1, ry2, rq3, ry13, ry23, em,
    asem, ssem, gsem, qsem, rsem, ss0, xs0, zs0, ys0, ss1, rs1, ss2, rs2, ss3, rs3, ss4, rs4,
):
    y, lane = lax.axis_index("grp"), lax.axis_index("lane")
    x, z, c = lax.div(lane, 8), mod4(lax.div(lane, 2)), lax.rem(lane, 2)

    def dev(x_, y_, z_, c_):
        return {"grp": y_, "lane": (x_ * 4 + z_) * 2 + c_}

    def send(src, dst, ss, rs, to):
        pltpu.make_async_remote_copy(
            src_ref=src, dst_ref=dst, send_sem=ss, recv_sem=rs, device_id=to, device_id_type=MESH
        ).start()

    def load(i):
        cols = pl.ds(pl.multiple_of(i * KW, KW), KW)
        return (
            pltpu.make_async_copy(s_hbm.at[cols, :], s.at[cols, :], ssem.at[i]),
            pltpu.make_async_copy(a_hbm.at[:, cols], a.at[:, cols], asem.at[i]),
        )

    for i in range(NK):
        for copy in load(i):
            copy.start()

    barrier = pltpu.get_barrier_semaphore()
    pl.semaphore_signal(barrier, inc=1, device_id=dev(x, y, z, 1 - c), device_id_type=MESH)

    def greet(d, carry):
        to = dev(mod4(x + lax.div(d, 4)), y, mod4(z + lax.rem(d, 4)), c)
        pl.semaphore_signal(barrier, inc=1, device_id=to, device_id_type=MESH)
        return carry

    lax.fori_loop(1, 16, greet, 0)
    for d in range(1, 4):
        pl.semaphore_signal(barrier, inc=1, device_id=dev(x, mod4(y + d), z, c), device_id_type=MESH)

    acc[...] = jnp.zeros_like(acc)

    def sample(i, carry):
        cols = pl.ds(pl.multiple_of(i * KW, KW), KW)
        for copy in load(i):
            copy.wait()
        acc[...] += jnp.dot(a[:, cols], s[cols, :], preferred_element_type=F32)
        return carry

    lax.fori_loop(0, NK, sample, 0)

    def mm(u, v):
        return jnp.dot(u, v, preferred_element_type=F32)

    def split(i, carry):
        g0, m = carry
        rows = pl.ds(pl.multiple_of(i * 256, 256), 256)
        v = acc[rows, :]
        hi = v.astype(BF16)
        rest = v - hi.astype(F32)
        mid = rest.astype(BF16)
        lo = (rest - mid.astype(F32)).astype(BF16)
        hit = hi.astype(F32).T.astype(BF16)
        ht[:, rows] = hit
        g0 = g0 + mm(hit, hi) + mm(mid.astype(F32).T.astype(BF16), mid)
        return g0, m + mm(hit, mid) + mm(hit, lo)

    zero = jnp.zeros((256, 256), F32)
    g0, m = lax.fori_loop(0, 4, split, (zero, zero))
    g[...] = g0 + m + m.T

    pl.semaphore_wait(barrier, 19)
    other = pl.ds(pl.multiple_of((1 - c) * 128, 128), 128)
    mine = pl.ds(pl.multiple_of(c * 128, 128), 128)
    core = dev(x, y, z, 1 - c)
    send(g.at[other, :], gh, gsem.at[0], gsem.at[1], core)

    def piece(x_, z_):
        return pl.ds(pl.multiple_of(c * 128 + (x_ * 4 + z_) * 8, 8), 8)

    def plane(d):
        return mod4(x + lax.div(d, 4)), mod4(z + lax.rem(d, 4))

    def scatter_gram(d, carry):
        x_, z_ = plane(d)
        send(g.at[piece(x_, z_), :], gr.at[d - 1], gsem.at[2], gsem.at[3], dev(x_, y, z_, c))
        return carry

    def order(i, k):
        dx, dz = (k + 1) % 4, mod4(i + k + 1)
        return dx, dz, mod4(x + dx), mod4(z + dz)

    def block(x_, z_, c_):
        lb = (x_ * 4 + z_) * 2 + c_
        return mm(ht[...], a[:, pl.ds(pl.multiple_of(lb * 256, 256), 256)])

    def give(i):
        for k in range(4):
            _, _, x_, z_ = order(i, k)
            b = block(x_, z_, 1 - c)
            q[x_, z_, 0] = b[:, :128]
            q[x_, z_, 1] = b[:, 128:]
        for k in range(4):
            _, _, x_, z_ = order(i, k)
            send(q.at[x_, z_], r.at[x_, z_], qsem.at[x_ * 4 + z_], rsem.at[x_ * 4 + z_], core)

    def own(i):
        for k in range(4):
            _, _, x_, z_ = order(i, k)
            b = block(x_, z_, c)
            p[x_, z_, 0] = b[:, :128]
            p[x_, z_, 1] = b[:, 128:]
        for k in range(4):
            _, _, x_, z_ = order(i, k)
            wait(r.at[x_, z_], rsem.at[x_ * 4 + z_])
            p[x_, z_] += r[x_, z_]

    half_x, half_z = (pl.ds(0, RX), pl.ds(RX, RZ))

    def quarter(y_):
        return lax.rem(y_, 2), pl.ds(pl.multiple_of(Y0 + lax.div(y_, 2) * HY, 8), HY)

    def to_x(z_, h, way):
        x_ = mod4(x + 1 + 2 * way)
        send(p.at[x_, z_, h, half_x, :], rx.at[way, z_, h], ss1.at[0], rs1.at[way], dev(x_, y, z, c))

    def to_z(x_, h, way):
        z_ = mod4(z + 1 + 2 * way)
        send(p.at[x_, z_, h, half_z, :], rz.at[way, x_, h], ss1.at[1], rs1.at[2 + way], dev(x, y, z_, c))

    def to_y(x_, z_, way):
        y_ = mod4(y + 1 + 2 * way)
        ch_, rows = quarter(y_)
        send(p.at[x_, z_, ch_, rows, :], ry.at[way, x_, z_], ss1.at[2], rs1.at[4 + way], dev(x, y_, z, c))

    def scatter(i):
        for k in range(4):
            dx, dz, x_, z_ = order(i, k)
            way_y = k // 2
            ch_, rows = quarter(mod4(y + 2))
            send(p.at[x_, z_, ch_, rows, :], qy.at[x_, z_], ss0.at[2], ys0.at[x_ * 4 + z_], dev(x, mod4(y + 1 + 2 * way_y), z, c))
            if dx == 2:
                for way in range(2):
                    to = dev(mod4(x + 1 + 2 * way), y, z, c)
                    send(p.at[x_, z_, way, half_x, :], qx.at[way, z_], ss0.at[0], xs0.at[way * 4 + z_], to)

            @pl.when(dz == 2)
            def _():
                for way in range(2):
                    to = dev(x, y, mod4(z + 1 + 2 * way), c)
                    send(p.at[x_, z_, way, half_z, :], qz.at[way, x_], ss0.at[1], zs0.at[way * 4 + x_], to)

        for k in range(4):
            dx, dz, x_, z_ = order(i, k)
            to_y(x_, z_, 1 - k // 2)
            if dx == 1 or dx == 3:
                to_x(z_, 1 - dx // 2, dx // 2)

            @pl.when(dz == 1)
            def _():
                to_z(x_, 1, 0)

            @pl.when(dz == 3)
            def _():
                to_z(x_, 0, 1)

    def relay(i, carry):
        for k in range(4):
            dx, dz, x_, z_ = order(i, k)
            if dx == 2:
                for way in range(2):
                    x_n = mod4(x + 1 + 2 * way)
                    wait(qx.at[way, z_], xs0.at[way * 4 + z_])
                    p[x_n, z_, way, half_x, :] += qx[way, z_]
                    to_x(z_, way, way)

            @pl.when(dz == 2)
            def _():
                for way in range(2):
                    z_n = mod4(z + 1 + 2 * way)
                    wait(qz.at[way, x_], zs0.at[way * 4 + x_])
                    p[x_, z_n, way, half_z, :] += qz[way, x_]
                    to_z(x_, way, way)

            way_y = k // 2
            ch_, rows = quarter(mod4(y + 1 + 2 * way_y))
            wait(qy.at[x_, z_], ys0.at[x_ * 4 + z_])
            p[x_, z_, ch_, rows, :] += qy[x_, z_]
            to_y(x_, z_, way_y)
        return carry

    def turn(i, carry):
        @pl.when(i < 4)
        def _():
            give(i)

        @pl.when(i == 1)
        def _():
            wait(gh, gsem.at[1])
            g[mine, :] += gh[...]
            lax.fori_loop(1, 16, scatter_gram, 0)

        @pl.when(i == 4)
        def _():
            wait(gr, gsem.at[3])
            gy[y] = g[piece(x, z), :] + jnp.sum(gr[...], axis=0)
            for d in range(1, 4):
                send(gy.at[y], gy.at[y], gsem.at[4], gsem.at[5], dev(x, mod4(y + d), z, c))
            scatter(2)

        @pl.when(i >= 1)
        def _():
            own(i - 1)

        @pl.when((i == 1) | (i == 2) | (i == 4))
        def _():
            scatter(i - 1)

        return carry

    lax.fori_loop(0, 5, turn, 0)

    def gather_gram(d, carry):
        x_, z_ = plane(d)
        send(gf.at[piece(x, z), :], gf.at[piece(x, z), :], gsem.at[6], gsem.at[7], dev(x_, y, z_, c))
        return carry

    def sum_groups():
        wait(gy.at[pl.ds(0, 3)], gsem.at[5])
        gf[piece(x, z), :] = (gy[0] + gy[1]) + (gy[2] + gy[3])
        lax.fori_loop(1, 16, gather_gram, 0)
        lax.fori_loop(0, 4, relay, 0)

    def swap_halves():
        wait(gf.at[pl.ds(0, 120), :], gsem.at[7])
        send(gf.at[mine, :], gf.at[mine, :], gsem.at[8], gsem.at[9], core)
        em[...] = jnp.zeros_like(em)

    def halves():
        wait(gf.at[pl.ds(0, 120), :], gsem.at[6])
        wait(gf.at[mine, :], gsem.at[8])
        wait(gf.at[other, :], gsem.at[9])

    def f(j):
        return lambda: factor_step(gf, em, j)

    plan = {0: (sum_groups, swap_halves), 1: (), 2: (halves, f(0), f(1)), 3: (f(2),), 4: (f(3),)}

    def slot(i):
        for step in plan[i]:
            step()

    slot(0)

    ch = lax.rem(y, 2)
    y0 = Y0 + lax.div(y, 2) * HY
    rows_y = pl.ds(pl.multiple_of(y0, 8), HY)
    rows_1 = pl.ds(pl.multiple_of(y0, 8), HY1)
    rows_2 = pl.ds(pl.multiple_of(y0 + HY1, 8), HY - HY1)
    rows_x, rows_z = pl.ds(0, RX), pl.ds(RX, RZ)
    for d in range(2):
        wait(rx.at[d], rs1.at[d])
    for k in range(4):
        p[x, k, :, rows_x, :] += rx[0, k] + rx[1, k]
    for d in range(1, 4):
        z_ = mod4(z + d)
        send(p.at[x, z_, :, rows_x, :], rx2.at[d - 1], ss2.at[d - 1], rs2.at[d - 1], dev(x, y, z_, c))
    for d in range(2):
        wait(rz.at[d], rs1.at[2 + d])
    for k in range(4):
        p[k, z, :, rows_z, :] += rz[0, k] + rz[1, k]
    for d in range(1, 4):
        x_ = mod4(x + d)
        send(p.at[x_, z, :, rows_z, :], rz2.at[d - 1], ss2.at[2 + d], rs2.at[2 + d], dev(x_, y, z, c))
    slot(1)
    for d in range(2):
        wait(ry.at[d], rs1.at[4 + d])
    for k in range(4):
        p[k, :, ch, rows_y, :] += ry[0, k] + ry[1, k]
    for d in range(1, 4):
        x_, z_ = mod4(x + d), mod4(z + d)
        send(p.at[x_, :, ch, rows_1, :], ry1.at[d - 1], ss2.at[5 + d], rs2.at[5 + d], dev(x_, y, z, c))
        send(p.at[:, z_, ch, rows_2, :], ry2.at[d - 1], ss2.at[8 + d], rs2.at[8 + d], dev(x, y, z_, c))

    slot(2)

    for d in range(3):
        wait(rx2.at[d], rs2.at[d])
    p[x, z, :, rows_x, :] += rx2[0] + rx2[1] + rx2[2]
    for d in range(3):
        wait(rz2.at[d], rs2.at[3 + d])
    p[x, z, :, rows_z, :] += rz2[0] + rz2[1] + rz2[2]
    for d in range(1, 4):
        y_ = mod4(y + d)
        rows = pl.ds(pl.multiple_of(lax.div(y_, 2) * HXZ, 8), HXZ)
        send(p.at[x, z, lax.rem(y_, 2), rows, :], rq3.at[d - 1], ss3.at[d - 1], rs3.at[d - 1], dev(x, y_, z, c))
    for d in range(3):
        wait(ry1.at[d], rs2.at[6 + d])
    p[x, :, ch, rows_1, :] += ry1[0] + ry1[1] + ry1[2]
    for d in range(1, 4):
        z_ = mod4(z + d)
        send(p.at[x, z_, ch, rows_1, :], ry13.at[d - 1], ss3.at[2 + d], rs3.at[2 + d], dev(x, y, z_, c))
    for d in range(3):
        wait(ry2.at[d], rs2.at[9 + d])
    p[:, z, ch, rows_2, :] += ry2[0] + ry2[1] + ry2[2]
    for d in range(1, 4):
        x_ = mod4(x + d)
        send(p.at[x_, z, ch, rows_2, :], ry23.at[d - 1], ss3.at[5 + d], rs3.at[5 + d], dev(x_, y, z, c))

    slot(3)

    rows_q = pl.ds(pl.multiple_of(lax.div(y, 2) * HXZ, 8), HXZ)
    for d in range(3):
        wait(rq3.at[d], rs3.at[d])
    cb[ch, rows_q, :] = p[x, z, ch, rows_q, :] + (rq3[0] + rq3[1] + rq3[2])
    for d in range(1, 4):
        send(cb.at[ch, rows_q, :], cb.at[ch, rows_q, :], ss4.at[d - 1], rs4.at[d - 1], dev(x, mod4(y + d), z, c))
    for d in range(3):
        wait(ry13.at[d], rs3.at[3 + d])
        wait(ry23.at[d], rs3.at[6 + d])
    cb[ch, rows_1, :] = p[x, z, ch, rows_1, :] + (ry13[0] + ry13[1] + ry13[2])
    cb[ch, rows_2, :] = p[x, z, ch, rows_2, :] + (ry23[0] + ry23[1] + ry23[2])
    for d in range(1, 4):
        send(cb.at[ch, rows_y, :], cb.at[ch, rows_y, :], ss4.at[d + 2], rs4.at[d + 2], dev(x, mod4(y + d), z, c))

    slot(4)

    def sent(t, carry):
        x_, z_ = lax.div(t, 4), lax.rem(t, 4)
        wait(q.at[x_, z_], qsem.at[t])
        return carry

    lax.fori_loop(0, 16, sent, 0)
    for k, (near, far) in enumerate(((rx, qx), (rz, qz), (ry, qy))):
        wait(far, ss0.at[k])
        wait(near, ss1.at[k])
    wait(gh, gsem.at[0])
    wait(gr, gsem.at[2])
    wait(gy.at[pl.ds(0, 3)], gsem.at[4])
    for d in range(3):
        wait(rx2.at[d], ss2.at[d])
        wait(rz2.at[d], ss2.at[3 + d])
        wait(ry1.at[d], ss2.at[6 + d])
        wait(ry2.at[d], ss2.at[9 + d])
        wait(rq3.at[d], ss3.at[d])
        wait(ry13.at[d], ss3.at[3 + d])
        wait(ry23.at[d], ss3.at[6 + d])
        wait(rq3.at[d], ss4.at[d])
        wait(cb.at[ch, rows_y, :], ss4.at[3 + d])
    for d in range(3):
        wait(rq3.at[d], rs4.at[d])
        wait(cb.at[ch, rows_y, :], rs4.at[3 + d])
    for h in range(2):
        out[:, 128 * h : 128 * h + 128] = mm32(em[...], cb[h])


def local(activations, sketch):
    dma = pltpu.SemaphoreType.DMA
    vmem = pltpu.VMEM
    return pl.pallas_call(
        kernel,
        out_shape=jax.ShapeDtypeStruct((256, 256), F32),
        in_specs=[pl.BlockSpec(memory_space=pl.ANY)] * 2,
        out_specs=pl.BlockSpec(memory_space=pltpu.VMEM),
        scratch_shapes=[
            vmem((1024, 8192), BF16), vmem((8192, 256), BF16), vmem((1024, 256), F32), vmem((256, 1024), BF16),
            vmem((256, 256), F32), vmem((128, 256), F32), vmem((15, 8, 256), F32), vmem((4, 8, 256), F32), vmem((256, 256), F32),
            vmem((4, 4, 2, 256, 128), F32), vmem((4, 4, 2, 256, 128), F32), vmem((4, 4, 2, 256, 128), F32), vmem((2, 256, 128), F32),
            vmem((2, 4, RX, 128), F32), vmem((2, 4, RZ, 128), F32), vmem((4, 4, HY, 128), F32),
            vmem((2, 4, 2, RX, 128), F32), vmem((2, 4, 2, RZ, 128), F32), vmem((2, 4, 4, HY, 128), F32),
            vmem((3, 2, RX, 128), F32), vmem((3, 2, RZ, 128), F32), vmem((3, 4, HY1, 128), F32), vmem((3, 4, HY - HY1, 128), F32),
            vmem((3, HXZ, 128), F32), vmem((3, HY1, 128), F32), vmem((3, HY - HY1, 128), F32), vmem((256, 256), F32),
            dma((NK,)), dma((NK,)), dma((10,)), dma((16,)), dma((16,)),
            dma((3,)), dma((8,)), dma((8,)), dma((16,)), dma((3,)), dma((6,)), dma((12,)), dma((12,)), dma((9,)), dma((9,)), dma((6,)), dma((6,)),
        ],
        compiler_params=pltpu.CompilerParams(collective_id=0, has_side_effects=True, vmem_limit_bytes=56 << 20),
        cost_estimate=pl.CostEstimate(flops=9_000_000_000, bytes_accessed=22_000_000, transcendentals=0),
    )(activations, sketch).T


def solution(mesh):
    return jax.shard_map(
        local,
        mesh=mesh,
        in_specs=(P(("grp", "lane"), None), P()),
        out_specs=P("lane", None),
        check_vma=False,
    )
```

```python
import functools

import jax
import jax.numpy as jnp
from jax import lax
from jax.experimental import pallas as pl
from jax.experimental.pallas import tpu as pltpu
from jax.sharding import PartitionSpec as P

MESH = pl.DeviceIdType.MESH
F32, BF16 = jnp.float32, jnp.bfloat16
NK, KW = 8, 1024
RX, RZ, RY = 80, 80, 96
NB = 64
RS = 32
Y0, HXZ, HS, HY, HY1 = RX + RZ, (RX + RZ) // 2 - RS, RS // 2, RY // 2, 24


def mod4(v):
    return lax.rem(v, 4)


def wait(ref, sem):
    pltpu.make_async_copy(ref, ref, sem).wait()


def panel(rows, q):
    n = len(rows)
    top = rows[q]
    wide = top.shape
    at = 8 * q

    def lanes(v, k):
        return jnp.broadcast_to(v[:, at + k:at + k + 1], wide)

    def subl(v, k):
        return jnp.broadcast_to(v[k:k + 1, :], wide)

    cols = [lanes(top, k) for k in range(8)]
    a = {(l, k): subl(cols[k], l) for k in range(8) for l in range(k, 8)}
    below = {i: [lanes(rows[i], k) for k in range(8)] for i in range(q + 1, n)}
    b = [subl(top, k) for k in range(8)]
    inv = []
    for k in range(8):
        rs = lax.rsqrt(a[k, k])
        inv.append(rs)
        for l in range(k + 1, 8):
            a[l, k] = a[l, k] * rs
        for m in range(k + 1, 8):
            for l in range(m, 8):
                a[l, m] = a[l, m] - a[l, k] * a[m, k]
        b[k] = b[k] * rs
        for l in range(k + 1, 8):
            b[l] = b[l] - a[l, k] * b[k]
    if q + 1 < n:
        d = [None] * 8
        for k in reversed(range(8)):
            v = b[k]
            for l in range(7, k, -1):
                v = v - a[l, k] * d[l]
            d[k] = v * inv[k]
        for i in range(q + 1, n):
            v = rows[i]
            for k in reversed(range(8)):
                v = v - below[i][k] * d[k]
            rows[i] = v
    sub = lax.broadcasted_iota(jnp.int32, wide, 0)
    out = b[0]
    for k in range(1, 8):
        out = jnp.where(sub == k, b[k], out)
    return out


def mm32(u, v):
    return jnp.dot(u, v, precision=lax.Precision.HIGHEST, preferred_element_type=F32)


def factor_step(gm, em, j):
    lo, hi = j * NB, (j + 1) * NB
    eye = (
        lax.broadcasted_iota(jnp.int32, (NB, NB), 0) == lax.broadcasted_iota(jnp.int32, (NB, NB), 1)
    ).astype(F32)
    m = jnp.concatenate([gm[lo:hi, lo:hi], eye], axis=1)
    rows = [m[8 * i : 8 * i + 8, :] for i in range(NB // 8)]
    w = jnp.concatenate([panel(rows, q) for q in range(NB // 8)], axis=0)[:, NB:]
    if j:
        em[lo:hi, 0:lo] = mm32(w, em[lo:hi, 0:lo])
    em[lo:hi, lo:hi] = w
    if hi < 256:
        t = mm32(w, gm[lo:hi, hi:256])
        tt = t.T
        gm[hi:256, hi:256] -= mm32(tt, t)
        em[hi:256, 0:hi] -= mm32(tt, em[lo:hi, 0:hi])


def kernel(
    a_hbm, s_hbm, out,
    a, s, acc, ht, g, gh, gr, gy, gf, q, r, p, cb,
    qx, qz, qy, rx, rz, ry, rx2, rz2, ry1, ry2, rq3, ry13, ry23, rxy, rzy, rxy3, rzy3, em,
    asem, ssem, gsem, qsem, rsem, ss0, xs0, zs0, ys0, ss1, rs1, ss2, rs2, ss3, rs3, ss4, rs4,
):
    y, lane = lax.axis_index("grp"), lax.axis_index("lane")
    x, z, c = lax.div(lane, 8), mod4(lax.div(lane, 2)), lax.rem(lane, 2)

    def dev(x_, y_, z_, c_):
        return {"grp": y_, "lane": (x_ * 4 + z_) * 2 + c_}

    def send(src, dst, ss, rs, to):
        pltpu.make_async_remote_copy(
            src_ref=src, dst_ref=dst, send_sem=ss, recv_sem=rs, device_id=to, device_id_type=MESH
        ).start()

    def load(i):
        cols = pl.ds(pl.multiple_of(i * KW, KW), KW)
        return (
            pltpu.make_async_copy(s_hbm.at[cols, :], s.at[cols, :], ssem.at[i]),
            pltpu.make_async_copy(a_hbm.at[:, cols], a.at[:, cols], asem.at[i]),
        )

    for i in range(NK):
        for copy in load(i):
            copy.start()

    barrier = pltpu.get_barrier_semaphore()
    pl.semaphore_signal(barrier, inc=1, device_id=dev(x, y, z, 1 - c), device_id_type=MESH)

    def greet(d, carry):
        to = dev(mod4(x + lax.div(d, 4)), y, mod4(z + lax.rem(d, 4)), c)
        pl.semaphore_signal(barrier, inc=1, device_id=to, device_id_type=MESH)
        return carry

    lax.fori_loop(1, 16, greet, 0)
    for d in range(1, 4):
        pl.semaphore_signal(barrier, inc=1, device_id=dev(x, mod4(y + d), z, c), device_id_type=MESH)

    acc[...] = jnp.zeros_like(acc)

    def sample(i, carry):
        cols = pl.ds(pl.multiple_of(i * KW, KW), KW)
        for copy in load(i):
            copy.wait()
        acc[...] += jnp.dot(a[:, cols], s[cols, :], preferred_element_type=F32)
        return carry

    lax.fori_loop(0, NK, sample, 0)

    def mm(u, v):
        return jnp.dot(u, v, preferred_element_type=F32)

    def split(i, carry):
        g0, m = carry
        rows = pl.ds(pl.multiple_of(i * 256, 256), 256)
        v = acc[rows, :]
        hi = v.astype(BF16)
        rest = v - hi.astype(F32)
        mid = rest.astype(BF16)
        lo = (rest - mid.astype(F32)).astype(BF16)
        hit = hi.astype(F32).T.astype(BF16)
        ht[:, rows] = hit
        g0 = g0 + mm(hit, hi) + mm(mid.astype(F32).T.astype(BF16), mid)
        return g0, m + mm(hit, mid) + mm(hit, lo)

    zero = jnp.zeros((256, 256), F32)
    g0, m = lax.fori_loop(0, 4, split, (zero, zero))
    g[...] = g0 + m + m.T

    pl.semaphore_wait(barrier, 19)
    other = pl.ds(pl.multiple_of((1 - c) * 128, 128), 128)
    mine = pl.ds(pl.multiple_of(c * 128, 128), 128)
    core = dev(x, y, z, 1 - c)
    send(g.at[other, :], gh, gsem.at[0], gsem.at[1], core)

    def piece(x_, z_):
        return pl.ds(pl.multiple_of(c * 128 + (x_ * 4 + z_) * 8, 8), 8)

    def plane(d):
        return mod4(x + lax.div(d, 4)), mod4(z + lax.rem(d, 4))

    def scatter_gram(d, carry):
        x_, z_ = plane(d)
        send(g.at[piece(x_, z_), :], gr.at[d - 1], gsem.at[2], gsem.at[3], dev(x_, y, z_, c))
        return carry

    def order(i, k):
        dx, dz = (k + 1) % 4, mod4(i + k + 1)
        return dx, dz, mod4(x + dx), mod4(z + dz)

    def block(x_, z_, c_):
        lb = (x_ * 4 + z_) * 2 + c_
        return mm(ht[...], a[:, pl.ds(pl.multiple_of(lb * 256, 256), 256)])

    def give(i):
        for k in range(4):
            _, _, x_, z_ = order(i, k)
            b = block(x_, z_, 1 - c)
            q[x_, z_, 0] = b[:, :128]
            q[x_, z_, 1] = b[:, 128:]
        for k in range(4):
            _, _, x_, z_ = order(i, k)
            send(q.at[x_, z_], r.at[x_, z_], qsem.at[x_ * 4 + z_], rsem.at[x_ * 4 + z_], core)

    def own(i):
        for k in range(4):
            _, _, x_, z_ = order(i, k)
            b = block(x_, z_, c)
            p[x_, z_, 0] = b[:, :128]
            p[x_, z_, 1] = b[:, 128:]
        for k in range(4):
            _, _, x_, z_ = order(i, k)
            wait(r.at[x_, z_], rsem.at[x_ * 4 + z_])
            p[x_, z_] += r[x_, z_]

    half_x, half_z = (pl.ds(0, RX), pl.ds(RX, RZ))

    def quarter(y_):
        return lax.rem(y_, 2), pl.ds(pl.multiple_of(Y0 + lax.div(y_, 2) * HY, 8), HY)

    def to_x(z_, h, way):
        x_ = mod4(x + 1 + 2 * way)
        send(p.at[x_, z_, h, half_x, :], rx.at[way, z_, h], ss1.at[0], rs1.at[way], dev(x_, y, z, c))

    def to_z(x_, h, way):
        z_ = mod4(z + 1 + 2 * way)
        send(p.at[x_, z_, h, half_z, :], rz.at[way, x_, h], ss1.at[1], rs1.at[2 + way], dev(x, y, z_, c))

    def to_y(x_, z_, way):
        y_ = mod4(y + 1 + 2 * way)
        ch_, rows = quarter(y_)
        send(p.at[x_, z_, ch_, rows, :], ry.at[way, x_, z_], ss1.at[2], rs1.at[4 + way], dev(x, y_, z, c))

    def scatter_far(i):
        for k in range(4):
            dx, dz, x_, z_ = order(i, k)
            way_y = k // 2
            ch_, rows = quarter(mod4(y + 2))
            send(p.at[x_, z_, ch_, rows, :], qy.at[x_, z_], ss0.at[2], ys0.at[x_ * 4 + z_], dev(x, mod4(y + 1 + 2 * way_y), z, c))
            if dx == 2:
                for way in range(2):
                    to = dev(mod4(x + 1 + 2 * way), y, z, c)
                    send(p.at[x_, z_, way, half_x, :], qx.at[way, z_], ss0.at[0], xs0.at[way * 4 + z_], to)

            @pl.when(dz == 2)
            def _():
                for way in range(2):
                    to = dev(x, y, mod4(z + 1 + 2 * way), c)
                    send(p.at[x_, z_, way, half_z, :], qz.at[way, x_], ss0.at[1], zs0.at[way * 4 + x_], to)

    def scatter_near(i):
        for k in range(4):
            dx, dz, x_, z_ = order(i, k)
            to_y(x_, z_, 1 - k // 2)
            if dx == 1 or dx == 3:
                to_x(z_, 1 - dx // 2, dx // 2)

            @pl.when(dz == 1)
            def _():
                to_z(x_, 1, 0)

            @pl.when(dz == 3)
            def _():
                to_z(x_, 0, 1)

    def relay(i, carry):
        for k in range(4):
            dx, dz, x_, z_ = order(i, k)
            if dx == 2:
                for way in range(2):
                    x_n = mod4(x + 1 + 2 * way)
                    wait(qx.at[way, z_], xs0.at[way * 4 + z_])
                    p[x_n, z_, way, half_x, :] += qx[way, z_]
                    to_x(z_, way, way)

            @pl.when(dz == 2)
            def _():
                for way in range(2):
                    z_n = mod4(z + 1 + 2 * way)
                    wait(qz.at[way, x_], zs0.at[way * 4 + x_])
                    p[x_, z_n, way, half_z, :] += qz[way, x_]
                    to_z(x_, way, way)

            way_y = k // 2
            ch_, rows = quarter(mod4(y + 1 + 2 * way_y))
            wait(qy.at[x_, z_], ys0.at[x_ * 4 + z_])
            p[x_, z_, ch_, rows, :] += qy[x_, z_]
            to_y(x_, z_, way_y)
        return carry

    def near(i, carry):
        scatter_near(i)
        return carry

    def turn(i, carry):
        @pl.when(i < 4)
        def _():
            give(i)

        @pl.when(i == 1)
        def _():
            wait(gh, gsem.at[1])
            g[mine, :] += gh[...]
            lax.fori_loop(1, 16, scatter_gram, 0)

        @pl.when(i == 4)
        def _():
            wait(gr, gsem.at[3])
            gy[y] = g[piece(x, z), :] + jnp.sum(gr[...], axis=0)
            for d in range(1, 4):
                send(gy.at[y], gy.at[y], gsem.at[4], gsem.at[5], dev(x, mod4(y + d), z, c))
            scatter_near(1)

        @pl.when(i >= 1)
        def _():
            own(i - 1)

            scatter_far(i - 1)

        @pl.when(i == 2)
        def _():
            scatter_near(0)

        return carry

    lax.fori_loop(0, 5, turn, 0)
    lax.fori_loop(2, 4, near, 0)

    def gather_gram(d, carry):
        x_, z_ = plane(d)
        send(gf.at[piece(x, z), :], gf.at[piece(x, z), :], gsem.at[6], gsem.at[7], dev(x_, y, z_, c))
        return carry

    def sum_groups():
        wait(gy.at[pl.ds(0, 3)], gsem.at[5])
        gf[piece(x, z), :] = (gy[0] + gy[1]) + (gy[2] + gy[3])
        lax.fori_loop(1, 16, gather_gram, 0)
        lax.fori_loop(0, 4, relay, 0)

    def swap_halves():
        wait(gf.at[pl.ds(0, 120), :], gsem.at[7])
        send(gf.at[mine, :], gf.at[mine, :], gsem.at[8], gsem.at[9], core)
        em[...] = jnp.zeros_like(em)

    def halves():
        wait(gf.at[pl.ds(0, 120), :], gsem.at[6])
        wait(gf.at[mine, :], gsem.at[8])
        wait(gf.at[other, :], gsem.at[9])

    def f(j):
        return lambda: factor_step(gf, em, j)

    plan = {0: (sum_groups, swap_halves), 1: (), 2: (halves, f(0), f(1)), 3: (f(2),), 4: (f(3),)}

    def slot(i):
        for step in plan[i]:
            step()

    slot(0)

    ch = lax.rem(y, 2)
    y0 = Y0 + lax.div(y, 2) * HY
    rows_y = pl.ds(pl.multiple_of(y0, 8), HY)
    rows_1 = pl.ds(pl.multiple_of(y0, 8), HY1)
    rows_2 = pl.ds(pl.multiple_of(y0 + HY1, 8), HY - HY1)
    rows_x, rows_z = pl.ds(0, RX), pl.ds(RX, RZ)
    rows_xz, rows_zx = pl.ds(RS, RX - RS), pl.ds(RX, RZ - RS)

    def strip(first, size, y_):
        return pl.ds(pl.multiple_of(first + lax.div(y_, 2) * size, 8), size)

    rows_xy, rows_zy, rows_q = strip(0, HS, y), strip(Y0 - RS, HS, y), strip(RS, HXZ, y)
    for d in range(2):
        wait(rx.at[d], rs1.at[d])
    for k in range(4):
        p[x, k, :, rows_x, :] += rx[0, k] + rx[1, k]
    for d in range(1, 4):
        y_, z_ = mod4(y + d), mod4(z + d)
        send(p.at[x, z_, :, rows_xz, :], rx2.at[d - 1], ss2.at[d - 1], rs2.at[d - 1], dev(x, y, z_, c))
        send(p.at[x, :, lax.rem(y_, 2), strip(0, HS, y_), :], rxy.at[d - 1], ss2.at[11 + d], rs2.at[11 + d], dev(x, y_, z, c))
    for d in range(2):
        wait(rz.at[d], rs1.at[2 + d])
    for k in range(4):
        p[k, z, :, rows_z, :] += rz[0, k] + rz[1, k]
    for d in range(1, 4):
        x_, y_ = mod4(x + d), mod4(y + d)
        send(p.at[x_, z, :, rows_zx, :], rz2.at[d - 1], ss2.at[2 + d], rs2.at[2 + d], dev(x_, y, z, c))
        send(p.at[:, z, lax.rem(y_, 2), strip(Y0 - RS, HS, y_), :], rzy.at[d - 1], ss2.at[14 + d], rs2.at[14 + d], dev(x, y_, z, c))
    slot(1)
    for d in range(2):
        wait(ry.at[d], rs1.at[4 + d])
    for k in range(4):
        p[k, :, ch, rows_y, :] += ry[0, k] + ry[1, k]
    for d in range(1, 4):
        x_, z_ = mod4(x + d), mod4(z + d)
        send(p.at[x_, :, ch, rows_1, :], ry1.at[d - 1], ss2.at[5 + d], rs2.at[5 + d], dev(x_, y, z, c))
        send(p.at[:, z_, ch, rows_2, :], ry2.at[d - 1], ss2.at[8 + d], rs2.at[8 + d], dev(x, y, z_, c))

    slot(2)

    for d in range(3):
        wait(rx2.at[d], rs2.at[d])
    p[x, z, :, rows_xz, :] += rx2[0] + rx2[1] + rx2[2]
    for d in range(3):
        wait(rz2.at[d], rs2.at[3 + d])
    p[x, z, :, rows_zx, :] += rz2[0] + rz2[1] + rz2[2]
    for d in range(1, 4):
        y_ = mod4(y + d)
        send(p.at[x, z, lax.rem(y_, 2), strip(RS, HXZ, y_), :], rq3.at[d - 1], ss3.at[d - 1], rs3.at[d - 1], dev(x, y_, z, c))
    for d in range(3):
        wait(rxy.at[d], rs2.at[12 + d])
    p[x, :, ch, rows_xy, :] += rxy[0] + rxy[1] + rxy[2]
    for d in range(1, 4):
        z_ = mod4(z + d)
        send(p.at[x, z_, ch, rows_xy, :], rxy3.at[d - 1], ss3.at[8 + d], rs3.at[8 + d], dev(x, y, z_, c))
    for d in range(3):
        wait(rzy.at[d], rs2.at[15 + d])
    p[:, z, ch, rows_zy, :] += rzy[0] + rzy[1] + rzy[2]
    for d in range(1, 4):
        x_ = mod4(x + d)
        send(p.at[x_, z, ch, rows_zy, :], rzy3.at[d - 1], ss3.at[11 + d], rs3.at[11 + d], dev(x_, y, z, c))
    for d in range(3):
        wait(ry1.at[d], rs2.at[6 + d])
    p[x, :, ch, rows_1, :] += ry1[0] + ry1[1] + ry1[2]
    for d in range(1, 4):
        z_ = mod4(z + d)
        send(p.at[x, z_, ch, rows_1, :], ry13.at[d - 1], ss3.at[2 + d], rs3.at[2 + d], dev(x, y, z_, c))
    for d in range(3):
        wait(ry2.at[d], rs2.at[9 + d])
    p[:, z, ch, rows_2, :] += ry2[0] + ry2[1] + ry2[2]
    for d in range(1, 4):
        x_ = mod4(x + d)
        send(p.at[x_, z, ch, rows_2, :], ry23.at[d - 1], ss3.at[5 + d], rs3.at[5 + d], dev(x_, y, z, c))

    slot(3)

    for rows, got, first in (
        (rows_q, rq3, 0), (rows_xy, rxy3, 9), (rows_zy, rzy3, 12), (rows_1, ry13, 3), (rows_2, ry23, 6),
    ):
        for d in range(3):
            wait(got.at[d], rs3.at[first + d])
        cb[ch, rows, :] = p[x, z, ch, rows, :] + (got[0] + got[1] + got[2])
        done = rows_y if got is ry23 else rows
        if got is not ry13:
            for d in range(1, 4):
                send(cb.at[ch, done, :], cb.at[ch, done, :], ss4.at[d - 1], rs4.at[d - 1], dev(x, mod4(y + d), z, c))
    slot(4)

    def sent(t, carry):
        x_, z_ = lax.div(t, 4), lax.rem(t, 4)
        wait(q.at[x_, z_], qsem.at[t])
        return carry

    lax.fori_loop(0, 16, sent, 0)
    for k, (near, far) in enumerate(((rx, qx), (rz, qz), (ry, qy))):
        wait(far, ss0.at[k])
        wait(near, ss1.at[k])
    wait(gh, gsem.at[0])
    wait(gr, gsem.at[2])
    wait(gy.at[pl.ds(0, 3)], gsem.at[4])
    for d in range(3):
        wait(rx2.at[d], ss2.at[d])
        wait(rz2.at[d], ss2.at[3 + d])
        wait(ry1.at[d], ss2.at[6 + d])
        wait(ry2.at[d], ss2.at[9 + d])
        wait(rq3.at[d], ss3.at[d])
        wait(ry13.at[d], ss3.at[3 + d])
        wait(ry23.at[d], ss3.at[6 + d])
        wait(rxy.at[d], ss2.at[12 + d])
        wait(rzy.at[d], ss2.at[15 + d])
        wait(rxy3.at[d], ss3.at[9 + d])
        wait(rzy3.at[d], ss3.at[12 + d])
        wait(cb.at[ch, pl.ds(0, 128), :], ss4.at[d])
    for d in range(3):
        wait(cb.at[ch, pl.ds(0, 128), :], rs4.at[d])
    for h in range(2):
        out[:, 128 * h : 128 * h + 128] = mm32(em[...], cb[h])


def local(activations, sketch):
    dma = pltpu.SemaphoreType.DMA
    vmem = pltpu.VMEM
    return pl.pallas_call(
        kernel,
        out_shape=jax.ShapeDtypeStruct((256, 256), F32),
        in_specs=[pl.BlockSpec(memory_space=pl.ANY)] * 2,
        out_specs=pl.BlockSpec(memory_space=pltpu.VMEM),
        scratch_shapes=[
            vmem((1024, 8192), BF16), vmem((8192, 256), BF16), vmem((1024, 256), F32), vmem((256, 1024), BF16),
            vmem((256, 256), F32), vmem((128, 256), F32), vmem((15, 8, 256), F32), vmem((4, 8, 256), F32), vmem((256, 256), F32),
            vmem((4, 4, 2, 256, 128), F32), vmem((4, 4, 2, 256, 128), F32), vmem((4, 4, 2, 256, 128), F32), vmem((2, 256, 128), F32),
            vmem((2, 4, RX, 128), F32), vmem((2, 4, RZ, 128), F32), vmem((4, 4, HY, 128), F32),
            vmem((2, 4, 2, RX, 128), F32), vmem((2, 4, 2, RZ, 128), F32), vmem((2, 4, 4, HY, 128), F32),
            vmem((3, 2, RX - RS, 128), F32), vmem((3, 2, RZ - RS, 128), F32), vmem((3, 4, HY1, 128), F32), vmem((3, 4, HY - HY1, 128), F32),
            vmem((3, HXZ, 128), F32), vmem((3, HY1, 128), F32), vmem((3, HY - HY1, 128), F32),
            vmem((3, 4, HS, 128), F32), vmem((3, 4, HS, 128), F32), vmem((3, HS, 128), F32), vmem((3, HS, 128), F32), vmem((256, 256), F32),
            dma((NK,)), dma((NK,)), dma((10,)), dma((16,)), dma((16,)),
            dma((3,)), dma((8,)), dma((8,)), dma((16,)), dma((3,)), dma((6,)), dma((18,)), dma((18,)), dma((15,)), dma((15,)), dma((3,)), dma((3,)),
        ],
        compiler_params=pltpu.CompilerParams(collective_id=0, has_side_effects=True, vmem_limit_bytes=56 << 20),
        cost_estimate=pl.CostEstimate(flops=9_000_000_000, bytes_accessed=22_000_000, transcendentals=0),
    )(activations, sketch).T


def solution(mesh):
    return jax.shard_map(
        local,
        mesh=mesh,
        in_specs=(P(("grp", "lane"), None), P()),
        out_specs=P("lane", None),
        check_vma=False,
    )
```

```python
import functools

import jax
import jax.numpy as jnp
from jax import lax
from jax.experimental import pallas as pl
from jax.experimental.pallas import tpu as pltpu
from jax.sharding import PartitionSpec as P

MESH = pl.DeviceIdType.MESH
F32, BF16 = jnp.float32, jnp.bfloat16
NK, KW = 8, 1024
RX, RZ, RY = 80, 80, 96
NB = 64
RS = 32
Y0, HXZ, HS, HY, HY1 = RX + RZ, (RX + RZ) // 2 - RS, RS // 2, RY // 2, 24


def mod4(v):
    return lax.rem(v, 4)


def wait(ref, sem):
    pltpu.make_async_copy(ref, ref, sem).wait()


def panel(rows, q):
    n = len(rows)
    top = rows[q]
    wide = top.shape
    at = 8 * q

    def lanes(v, k):
        return jnp.broadcast_to(v[:, at + k:at + k + 1], wide)

    def subl(v, k):
        return jnp.broadcast_to(v[k:k + 1, :], wide)

    cols = [lanes(top, k) for k in range(8)]
    a = {(l, k): subl(cols[k], l) for k in range(8) for l in range(k, 8)}
    below = {i: [lanes(rows[i], k) for k in range(8)] for i in range(q + 1, n)}
    b = [subl(top, k) for k in range(8)]
    inv = []
    for k in range(8):
        rs = lax.rsqrt(a[k, k])
        inv.append(rs)
        for l in range(k + 1, 8):
            a[l, k] = a[l, k] * rs
        for m in range(k + 1, 8):
            for l in range(m, 8):
                a[l, m] = a[l, m] - a[l, k] * a[m, k]
        b[k] = b[k] * rs
        for l in range(k + 1, 8):
            b[l] = b[l] - a[l, k] * b[k]
    if q + 1 < n:
        d = [None] * 8
        for k in reversed(range(8)):
            v = b[k]
            for l in range(7, k, -1):
                v = v - a[l, k] * d[l]
            d[k] = v * inv[k]
        for i in range(q + 1, n):
            v = rows[i]
            for k in reversed(range(8)):
                v = v - below[i][k] * d[k]
            rows[i] = v
    sub = lax.broadcasted_iota(jnp.int32, wide, 0)
    out = b[0]
    for k in range(1, 8):
        out = jnp.where(sub == k, b[k], out)
    return out


def mm32(u, v):
    return jnp.dot(u, v, precision=lax.Precision.HIGHEST, preferred_element_type=F32)


def factor_step(gm, em, j):
    lo, hi = j * NB, (j + 1) * NB
    eye = (
        lax.broadcasted_iota(jnp.int32, (NB, NB), 0) == lax.broadcasted_iota(jnp.int32, (NB, NB), 1)
    ).astype(F32)
    m = jnp.concatenate([gm[lo:hi, lo:hi], eye], axis=1)
    rows = [m[8 * i : 8 * i + 8, :] for i in range(NB // 8)]
    w = jnp.concatenate([panel(rows, q) for q in range(NB // 8)], axis=0)[:, NB:]
    if j:
        em[lo:hi, 0:lo] = mm32(w, em[lo:hi, 0:lo])
    em[lo:hi, lo:hi] = w
    if hi < 256:
        t = mm32(w, gm[lo:hi, hi:256])
        tt = t.T
        gm[hi:256, hi:256] -= mm32(tt, t)
        em[hi:256, 0:hi] -= mm32(tt, em[lo:hi, 0:hi])


def kernel(
    a_hbm, s_hbm, c_out, e_out,
    a, s, acc, ht, g, gh, gr, gy, gf, q, r, p, cb,
    qx, qz, qy, rx, rz, ry, rx2, rz2, ry1, ry2, rq3, ry13, ry23, rxy, rzy, rxy3, rzy3, em,
    asem, ssem, gsem, qsem, rsem, ss0, xs0, zs0, ys0, ss1, rs1, ss2, rs2, ss3, rs3, ss4, rs4,
):
    y, lane = lax.axis_index("grp"), lax.axis_index("lane")
    x, z, c = lax.div(lane, 8), mod4(lax.div(lane, 2)), lax.rem(lane, 2)

    def dev(x_, y_, z_, c_):
        return {"grp": y_, "lane": (x_ * 4 + z_) * 2 + c_}

    def send(src, dst, ss, rs, to):
        pltpu.make_async_remote_copy(
            src_ref=src, dst_ref=dst, send_sem=ss, recv_sem=rs, device_id=to, device_id_type=MESH
        ).start()

    def load(i):
        cols = pl.ds(pl.multiple_of(i * KW, KW), KW)
        return (
            pltpu.make_async_copy(s_hbm.at[cols, :], s.at[cols, :], ssem.at[i]),
            pltpu.make_async_copy(a_hbm.at[:, cols], a.at[:, cols], asem.at[i]),
        )

    for i in range(NK):
        for copy in load(i):
            copy.start()

    barrier = pltpu.get_barrier_semaphore()
    pl.semaphore_signal(barrier, inc=1, device_id=dev(x, y, z, 1 - c), device_id_type=MESH)

    def greet(d, carry):
        to = dev(mod4(x + lax.div(d, 4)), y, mod4(z + lax.rem(d, 4)), c)
        pl.semaphore_signal(barrier, inc=1, device_id=to, device_id_type=MESH)
        return carry

    lax.fori_loop(1, 16, greet, 0)
    for d in range(1, 4):
        pl.semaphore_signal(barrier, inc=1, device_id=dev(x, mod4(y + d), z, c), device_id_type=MESH)

    acc[...] = jnp.zeros_like(acc)

    def sample(i, carry):
        cols = pl.ds(pl.multiple_of(i * KW, KW), KW)
        for copy in load(i):
            copy.wait()
        acc[...] += jnp.dot(a[:, cols], s[cols, :], preferred_element_type=F32)
        return carry

    lax.fori_loop(0, NK, sample, 0)

    def mm(u, v):
        return jnp.dot(u, v, preferred_element_type=F32)

    def split(i, carry):
        g0, m = carry
        rows = pl.ds(pl.multiple_of(i * 256, 256), 256)
        v = acc[rows, :]
        hi = v.astype(BF16)
        rest = v - hi.astype(F32)
        mid = rest.astype(BF16)
        lo = (rest - mid.astype(F32)).astype(BF16)
        hit = hi.astype(F32).T.astype(BF16)
        ht[:, rows] = hit
        g0 = g0 + mm(hit, hi) + mm(mid.astype(F32).T.astype(BF16), mid)
        return g0, m + mm(hit, mid) + mm(hit, lo)

    zero = jnp.zeros((256, 256), F32)
    g0, m = lax.fori_loop(0, 4, split, (zero, zero))
    g[...] = g0 + m + m.T

    pl.semaphore_wait(barrier, 19)
    other = pl.ds(pl.multiple_of((1 - c) * 128, 128), 128)
    mine = pl.ds(pl.multiple_of(c * 128, 128), 128)
    core = dev(x, y, z, 1 - c)
    send(g.at[other, :], gh, gsem.at[0], gsem.at[1], core)

    def piece(x_, z_):
        return pl.ds(pl.multiple_of(c * 128 + (x_ * 4 + z_) * 8, 8), 8)

    def plane(d):
        return mod4(x + lax.div(d, 4)), mod4(z + lax.rem(d, 4))

    def scatter_gram(d, carry):
        x_, z_ = plane(d)
        send(g.at[piece(x_, z_), :], gr.at[d - 1], gsem.at[2], gsem.at[3], dev(x_, y, z_, c))
        return carry

    def order(i, k):
        dx, dz = (k + 1) % 4, mod4(i + k + 1)
        return dx, dz, mod4(x + dx), mod4(z + dz)

    def block(x_, z_, c_):
        lb = (x_ * 4 + z_) * 2 + c_
        return mm(ht[...], a[:, pl.ds(pl.multiple_of(lb * 256, 256), 256)])

    def give(i):
        for k in range(4):
            _, _, x_, z_ = order(i, k)
            b = block(x_, z_, 1 - c)
            q[x_, z_, 0] = b[:, :128]
            q[x_, z_, 1] = b[:, 128:]
        for k in range(4):
            _, _, x_, z_ = order(i, k)
            send(q.at[x_, z_], r.at[x_, z_], qsem.at[x_ * 4 + z_], rsem.at[x_ * 4 + z_], core)

    def own(i):
        for k in range(4):
            _, _, x_, z_ = order(i, k)
            b = block(x_, z_, c)
            p[x_, z_, 0] = b[:, :128]
            p[x_, z_, 1] = b[:, 128:]
        for k in range(4):
            _, _, x_, z_ = order(i, k)
            wait(r.at[x_, z_], rsem.at[x_ * 4 + z_])
            p[x_, z_] += r[x_, z_]

    half_x, half_z = (pl.ds(0, RX), pl.ds(RX, RZ))

    def quarter(y_):
        return lax.rem(y_, 2), pl.ds(pl.multiple_of(Y0 + lax.div(y_, 2) * HY, 8), HY)

    def to_x(z_, h, way):
        x_ = mod4(x + 1 + 2 * way)
        send(p.at[x_, z_, h, half_x, :], rx.at[way, z_, h], ss1.at[0], rs1.at[way], dev(x_, y, z, c))

    def to_z(x_, h, way):
        z_ = mod4(z + 1 + 2 * way)
        send(p.at[x_, z_, h, half_z, :], rz.at[way, x_, h], ss1.at[1], rs1.at[2 + way], dev(x, y, z_, c))

    def to_y(x_, z_, way):
        y_ = mod4(y + 1 + 2 * way)
        ch_, rows = quarter(y_)
        send(p.at[x_, z_, ch_, rows, :], ry.at[way, x_, z_], ss1.at[2], rs1.at[4 + way], dev(x, y_, z, c))

    def scatter_far(i):
        for k in range(4):
            dx, dz, x_, z_ = order(i, k)
            way_y = k // 2
            ch_, rows = quarter(mod4(y + 2))
            send(p.at[x_, z_, ch_, rows, :], qy.at[x_, z_], ss0.at[2], ys0.at[x_ * 4 + z_], dev(x, mod4(y + 1 + 2 * way_y), z, c))
            if dx == 2:
                for way in range(2):
                    to = dev(mod4(x + 1 + 2 * way), y, z, c)
                    send(p.at[x_, z_, way, half_x, :], qx.at[way, z_], ss0.at[0], xs0.at[way * 4 + z_], to)

            @pl.when(dz == 2)
            def _():
                for way in range(2):
                    to = dev(x, y, mod4(z + 1 + 2 * way), c)
                    send(p.at[x_, z_, way, half_z, :], qz.at[way, x_], ss0.at[1], zs0.at[way * 4 + x_], to)

    def scatter_near(i):
        for k in range(4):
            dx, dz, x_, z_ = order(i, k)
            to_y(x_, z_, 1 - k // 2)
            if dx == 1 or dx == 3:
                to_x(z_, 1 - dx // 2, dx // 2)

            @pl.when(dz == 1)
            def _():
                to_z(x_, 1, 0)

            @pl.when(dz == 3)
            def _():
                to_z(x_, 0, 1)

    def relay(i, carry):
        for k in range(4):
            dx, dz, x_, z_ = order(i, k)
            if dx == 2:
                for way in range(2):
                    x_n = mod4(x + 1 + 2 * way)
                    wait(qx.at[way, z_], xs0.at[way * 4 + z_])
                    p[x_n, z_, way, half_x, :] += qx[way, z_]
                    to_x(z_, way, way)

            @pl.when(dz == 2)
            def _():
                for way in range(2):
                    z_n = mod4(z + 1 + 2 * way)
                    wait(qz.at[way, x_], zs0.at[way * 4 + x_])
                    p[x_, z_n, way, half_z, :] += qz[way, x_]
                    to_z(x_, way, way)

            way_y = k // 2
            ch_, rows = quarter(mod4(y + 1 + 2 * way_y))
            wait(qy.at[x_, z_], ys0.at[x_ * 4 + z_])
            p[x_, z_, ch_, rows, :] += qy[x_, z_]
            to_y(x_, z_, way_y)
        return carry

    def near(i, carry):
        scatter_near(i)
        return carry

    def turn(i, carry):
        @pl.when(i < 4)
        def _():
            give(i)

        @pl.when(i == 1)
        def _():
            wait(gh, gsem.at[1])
            g[mine, :] += gh[...]
            lax.fori_loop(1, 16, scatter_gram, 0)

        @pl.when(i == 4)
        def _():
            wait(gr, gsem.at[3])
            gy[y] = g[piece(x, z), :] + jnp.sum(gr[...], axis=0)
            for d in range(1, 4):
                send(gy.at[y], gy.at[y], gsem.at[4], gsem.at[5], dev(x, mod4(y + d), z, c))
            scatter_near(1)

        @pl.when(i >= 1)
        def _():
            own(i - 1)

            scatter_far(i - 1)

        @pl.when(i == 2)
        def _():
            scatter_near(0)

        return carry

    lax.fori_loop(0, 5, turn, 0)
    lax.fori_loop(2, 4, near, 0)

    def gather_gram(d, carry):
        x_, z_ = plane(d)
        send(gf.at[piece(x, z), :], gf.at[piece(x, z), :], gsem.at[6], gsem.at[7], dev(x_, y, z_, c))
        return carry

    def sum_groups():
        wait(gy.at[pl.ds(0, 3)], gsem.at[5])
        gf[piece(x, z), :] = (gy[0] + gy[1]) + (gy[2] + gy[3])
        lax.fori_loop(1, 16, gather_gram, 0)
        lax.fori_loop(0, 4, relay, 0)

    def swap_halves():
        wait(gf.at[pl.ds(0, 120), :], gsem.at[7])
        send(gf.at[mine, :], gf.at[mine, :], gsem.at[8], gsem.at[9], core)
        em[...] = jnp.zeros_like(em)

    def halves():
        wait(gf.at[pl.ds(0, 120), :], gsem.at[6])
        wait(gf.at[mine, :], gsem.at[8])
        wait(gf.at[other, :], gsem.at[9])

    def f(j):
        return lambda: factor_step(gf, em, j)

    plan = {0: (sum_groups, swap_halves), 1: (), 2: (halves, f(0), f(1)), 3: (f(2),), 4: (f(3),)}

    def slot(i):
        for step in plan[i]:
            step()

    slot(0)

    ch = lax.rem(y, 2)
    y0 = Y0 + lax.div(y, 2) * HY
    rows_y = pl.ds(pl.multiple_of(y0, 8), HY)
    rows_1 = pl.ds(pl.multiple_of(y0, 8), HY1)
    rows_2 = pl.ds(pl.multiple_of(y0 + HY1, 8), HY - HY1)
    rows_x, rows_z = pl.ds(0, RX), pl.ds(RX, RZ)
    rows_xz, rows_zx = pl.ds(RS, RX - RS), pl.ds(RX, RZ - RS)

    def strip(first, size, y_):
        return pl.ds(pl.multiple_of(first + lax.div(y_, 2) * size, 8), size)

    rows_xy, rows_zy, rows_q = strip(0, HS, y), strip(Y0 - RS, HS, y), strip(RS, HXZ, y)
    for d in range(2):
        wait(rx.at[d], rs1.at[d])
    for k in range(4):
        p[x, k, :, rows_x, :] += rx[0, k] + rx[1, k]
    for d in range(1, 4):
        y_, z_ = mod4(y + d), mod4(z + d)
        send(p.at[x, z_, :, rows_xz, :], rx2.at[d - 1], ss2.at[d - 1], rs2.at[d - 1], dev(x, y, z_, c))
        send(p.at[x, :, lax.rem(y_, 2), strip(0, HS, y_), :], rxy.at[d - 1], ss2.at[11 + d], rs2.at[11 + d], dev(x, y_, z, c))
    for d in range(2):
        wait(rz.at[d], rs1.at[2 + d])
    for k in range(4):
        p[k, z, :, rows_z, :] += rz[0, k] + rz[1, k]
    for d in range(1, 4):
        x_, y_ = mod4(x + d), mod4(y + d)
        send(p.at[x_, z, :, rows_zx, :], rz2.at[d - 1], ss2.at[2 + d], rs2.at[2 + d], dev(x_, y, z, c))
        send(p.at[:, z, lax.rem(y_, 2), strip(Y0 - RS, HS, y_), :], rzy.at[d - 1], ss2.at[14 + d], rs2.at[14 + d], dev(x, y_, z, c))
    slot(1)
    for d in range(2):
        wait(ry.at[d], rs1.at[4 + d])
    for k in range(4):
        p[k, :, ch, rows_y, :] += ry[0, k] + ry[1, k]
    for d in range(1, 4):
        x_, z_ = mod4(x + d), mod4(z + d)
        send(p.at[x_, :, ch, rows_1, :], ry1.at[d - 1], ss2.at[5 + d], rs2.at[5 + d], dev(x_, y, z, c))
        send(p.at[:, z_, ch, rows_2, :], ry2.at[d - 1], ss2.at[8 + d], rs2.at[8 + d], dev(x, y, z_, c))

    slot(2)

    for d in range(3):
        wait(rx2.at[d], rs2.at[d])
    p[x, z, :, rows_xz, :] += rx2[0] + rx2[1] + rx2[2]
    for d in range(3):
        wait(rz2.at[d], rs2.at[3 + d])
    p[x, z, :, rows_zx, :] += rz2[0] + rz2[1] + rz2[2]
    for d in range(1, 4):
        y_ = mod4(y + d)
        send(p.at[x, z, lax.rem(y_, 2), strip(RS, HXZ, y_), :], rq3.at[d - 1], ss3.at[d - 1], rs3.at[d - 1], dev(x, y_, z, c))
    for d in range(3):
        wait(rxy.at[d], rs2.at[12 + d])
    p[x, :, ch, rows_xy, :] += rxy[0] + rxy[1] + rxy[2]
    for d in range(1, 4):
        z_ = mod4(z + d)
        send(p.at[x, z_, ch, rows_xy, :], rxy3.at[d - 1], ss3.at[8 + d], rs3.at[8 + d], dev(x, y, z_, c))
    for d in range(3):
        wait(rzy.at[d], rs2.at[15 + d])
    p[:, z, ch, rows_zy, :] += rzy[0] + rzy[1] + rzy[2]
    for d in range(1, 4):
        x_ = mod4(x + d)
        send(p.at[x_, z, ch, rows_zy, :], rzy3.at[d - 1], ss3.at[11 + d], rs3.at[11 + d], dev(x_, y, z, c))
    for d in range(3):
        wait(ry1.at[d], rs2.at[6 + d])
    p[x, :, ch, rows_1, :] += ry1[0] + ry1[1] + ry1[2]
    for d in range(1, 4):
        z_ = mod4(z + d)
        send(p.at[x, z_, ch, rows_1, :], ry13.at[d - 1], ss3.at[2 + d], rs3.at[2 + d], dev(x, y, z_, c))
    for d in range(3):
        wait(ry2.at[d], rs2.at[9 + d])
    p[:, z, ch, rows_2, :] += ry2[0] + ry2[1] + ry2[2]
    for d in range(1, 4):
        x_ = mod4(x + d)
        send(p.at[x_, z, ch, rows_2, :], ry23.at[d - 1], ss3.at[5 + d], rs3.at[5 + d], dev(x_, y, z, c))

    slot(3)

    for rows, got, first in (
        (rows_q, rq3, 0), (rows_xy, rxy3, 9), (rows_zy, rzy3, 12), (rows_1, ry13, 3), (rows_2, ry23, 6),
    ):
        for d in range(3):
            wait(got.at[d], rs3.at[first + d])
        cb[ch, rows, :] = p[x, z, ch, rows, :] + (got[0] + got[1] + got[2])
        done = rows_y if got is ry23 else rows
        if got is not ry13:
            for d in range(1, 4):
                send(cb.at[ch, done, :], cb.at[ch, done, :], ss4.at[d - 1], rs4.at[d - 1], dev(x, mod4(y + d), z, c))
    slot(4)
    e_out[...] = em[...].T

    def sent(t, carry):
        x_, z_ = lax.div(t, 4), lax.rem(t, 4)
        wait(q.at[x_, z_], qsem.at[t])
        return carry

    lax.fori_loop(0, 16, sent, 0)
    for k, (near, far) in enumerate(((rx, qx), (rz, qz), (ry, qy))):
        wait(far, ss0.at[k])
        wait(near, ss1.at[k])
    wait(gh, gsem.at[0])
    wait(gr, gsem.at[2])
    wait(gy.at[pl.ds(0, 3)], gsem.at[4])
    for d in range(3):
        wait(rx2.at[d], ss2.at[d])
        wait(rz2.at[d], ss2.at[3 + d])
        wait(ry1.at[d], ss2.at[6 + d])
        wait(ry2.at[d], ss2.at[9 + d])
        wait(rq3.at[d], ss3.at[d])
        wait(ry13.at[d], ss3.at[3 + d])
        wait(ry23.at[d], ss3.at[6 + d])
        wait(rxy.at[d], ss2.at[12 + d])
        wait(rzy.at[d], ss2.at[15 + d])
        wait(rxy3.at[d], ss3.at[9 + d])
        wait(rzy3.at[d], ss3.at[12 + d])
        wait(cb.at[ch, pl.ds(0, 128), :], ss4.at[d])
    for d in range(3):
        wait(cb.at[ch, pl.ds(0, 128), :], rs4.at[d])
    for h in range(2):
        c_out[128 * h : 128 * h + 128, :] = cb[h].T


def local(activations, sketch):
    dma = pltpu.SemaphoreType.DMA
    vmem = pltpu.VMEM
    cross, inverse = pl.pallas_call(
        kernel,
        out_shape=(jax.ShapeDtypeStruct((256, 256), F32),) * 2,
        in_specs=[pl.BlockSpec(memory_space=pl.ANY)] * 2,
        out_specs=[pl.BlockSpec(memory_space=pltpu.VMEM)] * 2,
        scratch_shapes=[
            vmem((1024, 8192), BF16), vmem((8192, 256), BF16), vmem((1024, 256), F32), vmem((256, 1024), BF16),
            vmem((256, 256), F32), vmem((128, 256), F32), vmem((15, 8, 256), F32), vmem((4, 8, 256), F32), vmem((256, 256), F32),
            vmem((4, 4, 2, 256, 128), F32), vmem((4, 4, 2, 256, 128), F32), vmem((4, 4, 2, 256, 128), F32), vmem((2, 256, 128), F32),
            vmem((2, 4, RX, 128), F32), vmem((2, 4, RZ, 128), F32), vmem((4, 4, HY, 128), F32),
            vmem((2, 4, 2, RX, 128), F32), vmem((2, 4, 2, RZ, 128), F32), vmem((2, 4, 4, HY, 128), F32),
            vmem((3, 2, RX - RS, 128), F32), vmem((3, 2, RZ - RS, 128), F32), vmem((3, 4, HY1, 128), F32), vmem((3, 4, HY - HY1, 128), F32),
            vmem((3, HXZ, 128), F32), vmem((3, HY1, 128), F32), vmem((3, HY - HY1, 128), F32),
            vmem((3, 4, HS, 128), F32), vmem((3, 4, HS, 128), F32), vmem((3, HS, 128), F32), vmem((3, HS, 128), F32), vmem((256, 256), F32),
            dma((NK,)), dma((NK,)), dma((10,)), dma((16,)), dma((16,)),
            dma((3,)), dma((8,)), dma((8,)), dma((16,)), dma((3,)), dma((6,)), dma((18,)), dma((18,)), dma((15,)), dma((15,)), dma((3,)), dma((3,)),
        ],
        compiler_params=pltpu.CompilerParams(collective_id=0, has_side_effects=True, vmem_limit_bytes=56 << 20),
        cost_estimate=pl.CostEstimate(flops=9_000_000_000, bytes_accessed=22_000_000, transcendentals=0),
    )(activations, sketch)
    return jnp.dot(cross, inverse, precision=lax.Precision.HIGHEST, preferred_element_type=F32)


def solution(mesh):
    return jax.shard_map(
        local,
        mesh=mesh,
        in_specs=(P(("grp", "lane"), None), P()),
        out_specs=P("lane", None),
        check_vma=False,
    )
```
